512 devices in a mesh: stream: 64 (over x, z_lo, core), span: 8 (over z_hi, y).
Axes of the slice: x: 4, y: 4, z: 16 (z_hi: 2, z_lo: 8; z = z_hi * 8 + z_lo), core: 2. Of those that a mesh axis runs over, the one named last changes fastest.
Arguments:
- adjoint: float32 [7, 384, 64, 1152], P(None, 'stream', 'span'), may hold values from -6 to 6
- source: bfloat16 [7, 384, 64, 1152], P(None, 'stream', 'span'), may hold values from -6 to 6
- stencil: float32 [384, 64, 768], P('stream', 'span'), may hold values from 0.1 to 0.4
- line_coupling: float32 [6, 192], replicated, may hold values from 0.5 to 2
- line_diag: float32 [6, 192], replicated, may hold values from 0.0005 to 4
- omega: float32 [1], replicated, may hold values from 0.1 to 0.4
- phase: float32 [1], replicated, may hold values from -3.140625 to 3.140625
- match_owner: int32 [64, 8, 48, 1], P('stream', 'span'), may hold values from 0 to 63, as said below
- match_row: int32 [64, 8, 48], P('stream', 'span'), may hold values from 0 to 47
- tile_live: int32 [64, 8], P('stream', 'span'), may hold values from 12 to 48
Outputs:
- updated: float32 [7, 384, 64, 1152], P(None, 'stream', 'span')
The draws below stay inside these ranges and needn't reach their ends.
Inputs may be any that keep to these rules, and one draw needn't show every extreme that they name: `match_owner`: for tile (i, j), every owner is (i + 32 + o) mod 64 with o from -3 to 4; in the lines of one tile no owner is named by more than 8 lines, and one owner is named by exactly 8.
All inputs are finite; a program needn't handle non-finite values.
Results may differ from the reference program's by a relative error of at most 0.0008.
Values may be sent and summed in bfloat16 or wider, within the bound.
No kernel may reach another device: no remote copies, remote signals or barrier semaphores. Data moves between devices by JAX's collectives and lax.ppermute only.
A program may use at most 128 MiB of HBM per device.

```python
import math
import jax
import jax.numpy as jnp
from jax import lax

NT = 7
NV = 6
L = 192
CX = 6
CZ = 8
CAP = 8
NX = 384
NZ = 64
ROWS = 48
N_STREAM = 64
N_SPAN = 8


def state_levels(key, floor_level, top_level, chosen_floor, chosen_top):
    key_levels, key_chosen, key_pick = jax.random.split(key, 3)
    common_level = jnp.exp(jax.random.uniform(key_levels, (NV,), jnp.float32, math.log(floor_level), math.log(top_level)))
    picked_level = jnp.exp(jax.random.uniform(key_chosen, (NV,), jnp.float32, math.log(chosen_floor), math.log(chosen_top)))
    picked_state = jax.random.randint(key_pick, (), 0, NV)
    return jnp.where(jnp.arange(NV, dtype=jnp.int32) == picked_state, picked_level, common_level)


def state_scales(levels):
    scales = jnp.minimum(1.0, levels + 0.003)
    return jnp.repeat(scales, L)


def draw_line_diag(key, part):
    levels = state_levels(key, 0.001, 2.0, 0.001, 2.0)
    key = jax.random.fold_in(key, 5)
    spread = jnp.exp(jax.random.uniform(key, (NV, L), jnp.float32, math.log(0.5), math.log(2.0)))
    return (levels[:, None] * spread).astype(jnp.float32)


def draw_adjoint(key, part):
    levels = state_levels(key, 0.001, 2.0, 0.001, 2.0)
    key = jax.random.fold_in(key, 7)
    values = jnp.clip(jax.random.normal(key, (NT, NX, NZ, NV * L), jnp.float32), -6.0, 6.0)
    return (values * state_scales(levels)).astype(jnp.float32)


def draw_source(key, part):
    levels = state_levels(key, 0.001, 2.0, 0.001, 2.0)
    key = jax.random.fold_in(key, 9)
    values = jnp.clip(jax.random.normal(key, (NT, NX, NZ, NV * L), jnp.float32), -6.0, 6.0)
    return (values * state_scales(levels)).astype(jnp.bfloat16)


def draw_match_owner(key, part):

    def one_tile(index):
        tile_key = jax.random.fold_in(jax.random.fold_in(key, 11), index)
        key_first, key_second, key_third = jax.random.split(tile_key, 3)
        fullest = jax.random.randint(key_first, (), 0, 8).astype(jnp.int32)
        places = jax.random.permutation(key_second, 7 * CAP)[:ROWS - CAP].astype(jnp.int32)
        others = (fullest + 1 + places // CAP) % 8
        offsets = jnp.concatenate([jnp.zeros((CAP,), jnp.int32) + fullest, others])
        shuffle = jax.random.permutation(key_third, ROWS)
        offsets = offsets[shuffle]
        stream_tile = index // N_SPAN
        return ((stream_tile + N_STREAM // 2 + offsets - 3) % N_STREAM).astype(jnp.int32)
    tiles = jax.vmap(one_tile)(jnp.arange(N_STREAM * N_SPAN, dtype=jnp.int32))
    return tiles.reshape(N_STREAM, N_SPAN, ROWS, 1).astype(jnp.int32)


def with_ends(entries, key, least, high):
    place = [jax.random.randint(jax.random.fold_in(key, axis), (), 0, length) for axis, length in enumerate(entries.shape)]
    longest = entries.shape.index(max(entries.shape))
    neighbour = place[:longest] + [(place[longest] + 1) % entries.shape[longest]] + place[longest + 1:]
    return entries.at[tuple(place)].set(least).at[tuple(neighbour)].set(high)


def shard_levels(stream_key, dims, pieces, smallest, top_value):
    def one(position, shards_of):
        steps = jax.random.uniform(jax.random.fold_in(jax.random.fold_in(stream_key, 6), position), (shards_of,), jnp.float32, smallest / len(pieces), top_value / len(pieces))
        return jnp.repeat(jnp.exp(steps), dims[position] // shards_of).reshape((-1,) + (1,) * (len(dims) - position - 1))

    level = one(*pieces[0])
    for cut in pieces[1:]:
        level = level * one(*cut)
    return level


def setup_inputs(seed: int = 0) -> dict:
    splits = jax.random.split(jax.random.key(seed), 11)
    return {
        "adjoint": draw_adjoint(jax.random.fold_in(splits[10], 71), 0),
        "source": draw_source(jax.random.fold_in(splits[10], 71), 0),
        "stencil": jnp.clip(0.1 + 0.3 * jax.random.uniform(splits[2], (NX, NZ, 4 * L), jnp.float32) ** shard_levels(splits[2], (NX, NZ, 4 * L), ((0, 64), (1, 8)), -0.2, 0.2), 0.1, 0.4),
        "line_coupling": jnp.clip(jax.random.uniform(splits[3], (NV, L), jnp.float32, 0.5, 2.0), 0.5, 2.0),
        "line_diag": draw_line_diag(jax.random.fold_in(splits[10], 71), 0),
        "omega": jnp.clip(jax.random.uniform(splits[5], (1,), jnp.float32, 0.1, 0.4), 0.1, 0.4),
        "phase": jnp.clip(jax.random.uniform(splits[6], (1,), jnp.float32, -3.140625, 3.140625), -3.140625, 3.140625),
        "match_owner": draw_match_owner(jax.random.fold_in(splits[10], 71), 0),
        "match_row": with_ends(jax.random.randint(splits[8], (N_STREAM, N_SPAN, ROWS), 0, ROWS), jax.random.fold_in(splits[8], 1), 0, ROWS - 1).astype(jnp.int32),
        "tile_live": with_ends(jax.random.randint(splits[9], (N_STREAM, N_SPAN), ROWS // 4, ROWS + 1), jax.random.fold_in(splits[9], 1), ROWS // 4, ROWS).astype(jnp.int32),
    }


def line_inverse(coupling, diagonal):
    states = coupling.shape[0]
    points = coupling.shape[1]
    previous = jnp.concatenate([jnp.zeros((states, 1), coupling.dtype), coupling[:, :-1]], axis=1)
    centre = previous + coupling + diagonal

    def pivot_step(carry, inputs):
        centre_now, before = inputs
        pivot = centre_now - before * before / carry
        return pivot, pivot

    _, pivots = lax.scan(pivot_step, jnp.ones_like(centre[:, 0]), (centre.T, previous.T))
    pivot_before = jnp.concatenate([jnp.ones_like(pivots[:1]), pivots[:-1]], axis=0)
    identity = jnp.eye(points, dtype=coupling.dtype)

    def forward_step(carry, inputs):
        unit_row, before, pivot_prev = inputs
        value = unit_row[None, :] + (before / pivot_prev)[:, None] * carry
        return value, value

    start = jnp.zeros((states, points), coupling.dtype)
    _, lowered = lax.scan(forward_step, start, (identity, previous.T, pivot_before))

    def backward_step(carry, inputs):
        lowered_row, link, pivot = inputs
        value = (lowered_row + link[:, None] * carry) / pivot[:, None]
        return value, value

    _, solved = lax.scan(backward_step, start, (lowered, coupling.T, pivots), reverse=True)
    return solved.transpose(1, 0, 2)


def spectral_matrix(count):
    index = jnp.arange(count, dtype=jnp.int32)
    offset = index[:, None] - index[None, :]
    parity = jnp.where(offset % 2 == 0, 1.0, -1.0).astype(jnp.float32)
    sines = jnp.sin(jnp.pi * offset.astype(jnp.float32) / count)
    denominator = jnp.where(offset == 0, 1.0, sines)
    return jnp.where(offset == 0, 0.0, 0.5 * parity / denominator).astype(jnp.float32)


def shift_matrix(count, angle):
    index = jnp.arange(count, dtype=jnp.int32)
    offset = (index[:, None] - index[None, :]).astype(jnp.float32)
    total = jnp.ones((count, count), jnp.float32)
    for harmonic in range(1, (count - 1) // 2 + 1):
        total = total + 2.0 * jnp.cos(harmonic * (2.0 * jnp.pi * offset / count + angle))
    return total / count


def reference(adjoint, source, stencil, line_coupling, line_diag, omega, phase, match_owner, match_row, tile_live):
    highest = lax.Precision.HIGHEST
    inverse = line_inverse(line_coupling, line_diag)
    spectral = spectral_matrix(NT)
    shifted = shift_matrix(NT, phase[0])
    xpos = jnp.arange(NX, dtype=jnp.int32)
    zpos = jnp.arange(NZ, dtype=jnp.int32)
    tile_count = tile_live[(xpos // CX)[:, None], (zpos // CZ)[None, :]]
    local_index = (xpos % CX)[:, None] * CZ + (zpos % CZ)[None, :]
    living = (local_index < tile_count).astype(jnp.float32)
    owner_grid = match_owner[..., 0].reshape(N_STREAM, N_SPAN, CX, CZ).transpose(0, 2, 1, 3).reshape(NX, NZ)
    row_grid = match_row.reshape(N_STREAM, N_SPAN, CX, CZ).transpose(0, 2, 1, 3).reshape(NX, NZ)
    partner_x = owner_grid * CX + row_grid // CZ
    partner_z = (zpos // CZ)[None, :] * CZ + row_grid % CZ
    boundary = adjoint[..., L - 1::L]
    picked = boundary[:, partner_x, partner_z, :]
    ghost = jnp.einsum("tm,mxzv->txzv", shifted, picked, precision=highest)
    rounded = lax.optimization_barrier(adjoint.astype(jnp.bfloat16))

    def per_state(state):
        field = lax.dynamic_slice_in_dim(adjoint, state * L, L, 3)
        right = lax.dynamic_slice_in_dim(source, state * L, L, 3).astype(jnp.float32)
        near = lax.dynamic_slice_in_dim(rounded, state * L, L, 3).astype(jnp.float32)
        padded = jnp.pad(near, ((0, 0), (1, 1), (1, 1), (0, 0)))
        neighbours = stencil[None, :, :, 0:L] * padded[:, :-2, 1:-1]
        neighbours = neighbours + stencil[None, :, :, L:2 * L] * padded[:, 2:, 1:-1]
        neighbours = neighbours + stencil[None, :, :, 2 * L:3 * L] * padded[:, 1:-1, :-2]
        neighbours = neighbours + stencil[None, :, :, 3 * L:4 * L] * padded[:, 1:-1, 2:]
        coupling = lax.dynamic_index_in_dim(line_coupling, state, 0, keepdims=False)
        diagonal = lax.dynamic_index_in_dim(line_diag, state, 0, keepdims=False)
        previous = jnp.concatenate([jnp.zeros((1,), coupling.dtype), coupling[:-1]])
        centre = previous + coupling + diagonal
        ghost_state = lax.dynamic_index_in_dim(ghost, state, 3, keepdims=False)
        field_prev = jnp.concatenate([jnp.zeros_like(field[..., :1]), field[..., :-1]], axis=3)
        field_next = jnp.concatenate([field[..., 1:], ghost_state[..., None]], axis=3)
        mixing = jnp.einsum("mt,mxzl->txzl", spectral, field, precision=highest)
        applied = centre * field - previous * field_prev - coupling * field_next + omega[0] * mixing - neighbours
        residual = right - applied
        inverse_state = lax.dynamic_index_in_dim(inverse, state, 0, keepdims=False)
        correction = jnp.einsum("lm,txzm->txzl", inverse_state, residual, precision=highest)
        return field + living[None, :, :, None] * correction

    stacked = lax.map(per_state, jnp.arange(NV, dtype=jnp.int32))
    return stacked.transpose(1, 2, 3, 0, 4).reshape(NT, NX, NZ, NV * L)
```

```python
import functools
import math

import jax
import jax.numpy as jnp
from jax import lax
from jax.experimental import pallas as pl
from jax.experimental.pallas import tpu as pltpu
from jax.sharding import PartitionSpec as P

F32 = jnp.float32
BF16 = jnp.bfloat16
LANES = 128
HALF = 64
REACH = 3
OWNERS = 8


def iota(shape, dim):
    return lax.broadcasted_iota(jnp.int32, shape, dim)


def split(value):
    high = value.astype(BF16)
    return high, (value - high.astype(F32)).astype(BF16)


def edge_kernel(dims, u_ref, west_ref, east_ref, south_ref, north_ref, rim_ref):
    times, cx, cz, pairs = dims
    rows = cx * cz
    width = u_ref.shape[1]
    take = lambda t, x: u_ref[t * rows + x * cz : t * rows + x * cz + cz, :]
    west_ref[...] = jnp.concatenate([take(t, 0) for t in range(times)], 0).astype(BF16)
    east_ref[...] = jnp.concatenate([take(t, cx - 1) for t in range(times)], 0).astype(BF16)
    sub = iota((8, width), 0)
    for ref, z in ((south_ref, 0), (north_ref, cz - 1)):
        tiles = []
        for x in range(cx):
            tile = jnp.zeros((8, width), F32)
            for t in range(times):
                at = t * rows + x * cz + z
                tile = jnp.where(sub == t, u_ref[at : at + 1, :], tile)
            tiles.append(tile)
        ref[...] = jnp.concatenate(tiles, 0).astype(BF16)
    lane = iota((rows, LANES), 1)
    inner = lane % HALF
    found = jnp.zeros((rows, LANES), F32)
    for t in range(times):
        for pair in range(pairs):
            base = pair * 3 * LANES
            block = slice(t * rows, (t + 1) * rows)
            first = u_ref[block, base + LANES : base + 2 * LANES]
            second = u_ref[block, base + 2 * LANES : base + 3 * LANES]
            both = jnp.where(lane < HALF, first, second)
            spot = t * pairs + pair
            both = pltpu.roll(both, (spot - (HALF - 1)) % LANES, 1)
            found = jnp.where(inner == spot, both, found)
    high = found.astype(BF16).astype(F32)
    rest = found - high
    middle = rest.astype(BF16).astype(F32)
    low = rest - middle
    span = times * pairs
    rim = high + pltpu.roll(middle, span, 1) + pltpu.roll(low, 2 * span, 1)
    rim_ref[...] = rim.astype(BF16)


def scan_products(matrix, lane, points, backward):
    a, b, c, d = matrix
    step = 1
    while step < points:
        shift = (lane.shape[1] - step) if backward else step
        inside = (lane < points - step) if backward else (lane >= step)
        e = jnp.where(inside, pltpu.roll(a, shift, 1), 1.0)
        f = jnp.where(inside, pltpu.roll(b, shift, 1), 0.0)
        g = jnp.where(inside, pltpu.roll(c, shift, 1), 0.0)
        h = jnp.where(inside, pltpu.roll(d, shift, 1), 1.0)
        a, b, c, d = a * e + b * g, a * f + b * h, c * e + d * g, c * f + d * h
        scale = 1.0 / (a + b + c + d)
        a, b, c, d = a * scale, b * scale, c * scale, d * scale
        step *= 2
    return a / c


def local_kernel(
    dims,
    omega_ref,
    phase_ref,
    live_ref,
    place_ref,
    u_ref,
    source_ref,
    stencil_ref,
    coupling_ref,
    diag_ref,
    owner_ref,
    row_ref,
    work_ref,
    green_ref,
    shift_ref,
    pick_ref,
    rimw_ref,
    couple_s,
    diag_s,
    green_row,
    sum_row,
    green_col,
    sum_col,
    face_s,
    round_s,
):
    times, cx, cz, pairs, points, count = dims
    rows = cx * cz
    span = times * pairs
    pair_now = pl.program_id(0)
    wide = couple_s.shape[1]

    @pl.when(pair_now == 0)
    def prepare():
        states = coupling_ref.shape[0]
        lane = iota((8, wide), 1)
        couple_s[...] = jnp.ones_like(couple_s)
        diag_s[...] = jnp.ones_like(diag_s)
        couple_s[0:states, 0:points] = coupling_ref[...]
        diag_s[0:states, 0:points] = diag_ref[...]
        link = couple_s[...]
        diag = diag_s[...]
        before = jnp.where(lane == 0, 0.0, pltpu.roll(link, 1, 1))
        one = jnp.ones_like(link)
        e = scan_products((diag + before, diag * before, one, before), lane, points, False)
        inside = lane < points
        matrix = (
            jnp.where(inside, diag + link, 1.0),
            jnp.where(inside, diag * link, 0.0),
            jnp.where(inside, one, 0.0),
            jnp.where(inside, link, 1.0),
        )
        f = jnp.where(inside, scan_products(matrix, lane, points, True), 1.0)
        e_before = jnp.where(lane == 0, 1.0, pltpu.roll(e, 1, 1))
        e_before = jnp.where(inside, e_before, 1.0)
        green = 1.0 / (before * e_before / (before + e_before) + f)
        decay = jnp.log(1.0 + f / jnp.where(lane == 0, 1.0, before))
        decay = jnp.where((lane == 0) | (lane >= points), 0.0, decay)
        step = 1
        while step < points:
            decay = decay + jnp.where(lane >= step, pltpu.roll(decay, step, 1), 0.0)
            step *= 2
        odd = iota((8, wide), 0) % 2 == 1
        green = jnp.where(odd, pltpu.roll(green, HALF, 1), green)
        decay = jnp.where(odd, pltpu.roll(decay, HALF, 1), decay)
        green_row[...] = green
        sum_row[...] = decay
        green_col[...] = green.T
        sum_col[...] = decay.T

        low = iota((rows, LANES), 1) < HALF
        z = iota((rows, 3 * LANES), 0) % cz
        for way in range(4):
            at = way // 2 * 3 * LANES
            t0, t1, t2 = (stencil_ref[:, at + k * LANES : at + (k + 1) * LANES] for k in range(3))
            if way % 2 == 0:
                swap = pltpu.roll(t0, HALF, 1)
                tiles = (t0, jnp.where(low, t1, swap), jnp.where(low, swap, pltpu.roll(t1, HALF, 1)))
            else:
                swap = pltpu.roll(t2, HALF, 1)
                other = pltpu.roll(t1, HALF, 1)
                tiles = (jnp.where(low, other, swap), jnp.where(low, swap, t1), t2)
            face = jnp.concatenate(tiles, 1)
            if way == 0:
                rimw_ref[0:cz, :] = face[0:cz]
            elif way == 1:
                rimw_ref[cz : 2 * cz, :] = face[rows - cz :]
            elif way == 2:
                rimw_ref[2 * cz : 2 * cz + rows, :] = jnp.where(z == 0, face, 0.0)
                face = jnp.where(z == 0, 0.0, face)
            else:
                rimw_ref[2 * cz + rows : 2 * cz + 2 * rows, :] = jnp.where(z == cz - 1, face, 0.0)
                face = jnp.where(z == cz - 1, 0.0, face)
            face_s[way * rows : (way + 1) * rows, :] = face

        slot = owner_ref[...] - place_ref[0] + (count // 2 + REACH)
        slot = jnp.where(slot < 0, slot + count, slot)
        slot = jnp.where(slot >= count, slot - count, slot)
        diagonal = iota((rows, rows), 0) == iota((rows, rows), 1)
        target = jnp.sum(jnp.where(diagonal, row_ref[...].astype(F32), 0.0), axis=1, keepdims=True)
        target = target.astype(jnp.int32)
        wanted = slot * rows + target
        cell = iota((rows, OWNERS * rows), 1)
        pick_ref[...] = jnp.where(cell == wanted, 1.0, 0.0).astype(BF16)

        left = iota((LANES, LANES), 0)
        right = iota((LANES, LANES), 1)
        left_in = left % HALF
        right_in = right % HALF
        left_in_part = left_in % span
        offset = right_in // pairs - left_in_part // pairs
        angle = (2.0 * math.pi / times) * offset.astype(F32)
        total = jnp.ones((LANES, LANES), F32)
        for harmonic in range(1, (times - 1) // 2 + 1):
            total = total + 2.0 * jnp.cos(harmonic * (angle + phase_ref[0]))
        ok = (left // HALF != right // HALF) & (left_in_part % pairs == right_in % pairs)
        ok = ok & (right_in < span) & (left_in < 3 * span)
        high, low_part = split(jnp.where(ok, total / times, 0.0))
        shift_ref[0:LANES, :] = high
        shift_ref[LANES : 2 * LANES, :] = low_part

    for half in range(2):
        state = 2 * pair_now + half
        first = half * HALF
        g_row = green_row[pl.ds(state, 1), :]
        s_row = sum_row[pl.ds(state, 1), :]
        pick = iota((wide, 8), 1) == state
        g_col = jnp.sum(jnp.where(pick, green_col[...], 0.0), axis=1, keepdims=True)
        s_col = jnp.sum(jnp.where(pick, sum_col[...], 0.0), axis=1, keepdims=True)
        k = iota((wide, wide), 0)
        n = iota((wide, wide), 1)
        full = jnp.exp(-jnp.abs(s_col - s_row)) * jnp.where(k <= n, g_col, g_row)
        at_end = first + points - 1
        lane = iota((1, wide), 1)
        s_end = jnp.sum(jnp.where(lane == at_end, s_row, 0.0), axis=1, keepdims=True)
        link = couple_s[pl.ds(state, 1), :]
        c_end = jnp.sum(jnp.where(lane == points - 1, link, 0.0), axis=1, keepdims=True)
        last = c_end * jnp.exp(-jnp.abs(s_end - s_row)) * g_row
        inside_k = (k >= first) & (k < first + points)
        inside_n = (n >= first) & (n < first + points)
        inner = k % HALF
        added = (inner < span) & (inner % pairs == pair_now)
        full = jnp.where(inside_k, full, jnp.where(added, last, 0.0))
        full = jnp.where(inside_n, full, 0.0)
        high, low_part = split(full)
        green_ref[0, 2 * half] = high
        green_ref[0, 2 * half + 1] = low_part

    round_s[...] = u_ref[...].astype(BF16).astype(F32)
    omega = omega_ref[0]
    live = live_ref[0]
    z = iota((cz, 3 * LANES), 0)
    weights = []
    for n in range(1, (times - 1) // 2 + 1):
        weights.append(omega * (0.5 * (-1.0) ** n / math.sin(math.pi * n / times)))
    for x in range(cx):
        west, east, south, north = (
            face_s[way * rows + x * cz : way * rows + (x + 1) * cz, :] for way in range(4)
        )
        for t in range(times):
            at = lambda tt, xx: slice((tt % times) * rows + xx * cz, (tt % times) * rows + (xx + 1) * cz)
            here = round_s[at(t, x), :]
            value = source_ref[t, x].astype(F32)
            value += south * pltpu.roll(here, 1, 0) + north * pltpu.roll(here, cz - 1, 0)
            if x > 0:
                value += west * round_s[at(t, x - 1), :]
            if x < cx - 1:
                value += east * round_s[at(t, x + 1), :]
            for n, weight in enumerate(weights, 1):
                value -= weight * (u_ref[at(t + n, x), :] - u_ref[at(t - n, x), :])
            work_ref[at(t, x), :] = jnp.where(z + x * cz < live, value, u_ref[at(t, x), :])


def finish_kernel(dims, groups, live_ref, *refs):
    times, cx, cz, pairs, points = dims
    rim_refs = refs[:groups]
    (
        work_ref,
        green_ref,
        shift_ref,
        pick_ref,
        rimw_ref,
        west_ref,
        east_ref,
        south_ref,
        north_ref,
        out_ref,
        rim_s,
        ghost_s,
        south_s,
        north_s,
        high_s,
        low_s,
    ) = refs[groups:]
    rows = cx * cz

    @pl.when(pl.program_id(0) == 0)
    def ghosts():
        at = 0
        for ref in rim_refs:
            rim_s[at : at + ref.shape[0], :] = ref[...]
            at += ref.shape[0]
        picked = jnp.dot(pick_ref[...], rim_s[...], preferred_element_type=F32).astype(BF16)
        ghost = jnp.dot(picked, shift_ref[0:LANES, :], preferred_element_type=F32)
        ghost += jnp.dot(picked, shift_ref[LANES : 2 * LANES, :], preferred_element_type=F32)
        ghost_s[...] = ghost

    west = west_ref[...].astype(F32)
    east = east_ref[...].astype(F32)
    south_s[...] = south_ref[...].astype(F32)
    north_s[...] = north_ref[...].astype(F32)
    lane = iota((cz, LANES), 1)
    inner = lane % HALF
    low_half = lane < HALF
    for t in range(times):
        mine = (inner >= t * pairs) & (inner < (t + 1) * pairs)
        even, odd = [], []
        for x in range(cx):
            at = t * rows + x * cz
            value = work_ref[at : at + cz, :]
            if x == 0:
                value += rimw_ref[0:cz, :] * west[t * cz : (t + 1) * cz]
            if x == cx - 1:
                value += rimw_ref[cz : 2 * cz, :] * east[t * cz : (t + 1) * cz]
            south = rimw_ref[2 * cz + x * cz : 2 * cz + (x + 1) * cz, :]
            north = rimw_ref[2 * cz + rows + x * cz : 2 * cz + rows + (x + 1) * cz, :]
            value += south * south_s[x * 8 + t : x * 8 + t + 1, :]
            value += north * north_s[x * 8 + t : x * 8 + t + 1, :]
            ghost = jnp.where(mine, ghost_s[x * cz : (x + 1) * cz, :], 0.0)
            mid = value[:, LANES : 2 * LANES]
            even.append(jnp.concatenate([value[:, :LANES], jnp.where(low_half, mid, ghost)], 1))
            odd.append(jnp.concatenate([jnp.where(low_half, ghost, mid), value[:, 2 * LANES :]], 1))
        for half, pieces in ((0, even), (1, odd)):
            high, low = split(jnp.concatenate(pieces, 0))
            high_s[half, t * rows : (t + 1) * rows, :] = high
            low_s[half, t * rows : (t + 1) * rows, :] = low
    products = []
    for half in range(2):
        high = high_s[half]
        g_high = green_ref[0, 2 * half]
        total = jnp.dot(high, g_high, preferred_element_type=F32)
        total += jnp.dot(high, green_ref[0, 2 * half + 1], preferred_element_type=F32)
        total += jnp.dot(low_s[half], g_high, preferred_element_type=F32)
        products.append(total)
    even, odd = products
    tiles = (even[:, :LANES], even[:, LANES:] + odd[:, :LANES], odd[:, LANES:])
    live = live_ref[0]
    shape = out_ref.shape[:1] + (LANES,)
    alive = iota(shape, 0) % rows < live
    for k, tile in enumerate(tiles):
        lanes = slice(k * LANES, (k + 1) * LANES)
        out_ref[:, lanes] = jnp.where(alive, tile, work_ref[:, lanes])


def around(count, offset):
    return [((i + offset) % count, i) for i in range(count)]


def body(
    adjoint,
    source,
    stencil,
    line_coupling,
    line_diag,
    omega,
    phase,
    match_owner,
    match_row,
    tile_live,
):
    times, cx, cz, width = adjoint.shape
    states, points = line_coupling.shape
    pairs = states // 2
    rows = cx * cz
    lines = times * rows
    count = lax.axis_size("stream")
    spans = lax.axis_size("span")
    wide = 2 * LANES
    u = adjoint.reshape(lines, width)
    vmem = pl.BlockSpec(memory_space=pltpu.VMEM)
    smem = pl.BlockSpec(memory_space=pltpu.SMEM)
    west, east, south, north, rim = pl.pallas_call(
        functools.partial(edge_kernel, (times, cx, cz, pairs)),
        out_shape=(
            jax.ShapeDtypeStruct((times * cz, width), BF16),
            jax.ShapeDtypeStruct((times * cz, width), BF16),
            jax.ShapeDtypeStruct((cx * 8, width), BF16),
            jax.ShapeDtypeStruct((cx * 8, width), BF16),
            jax.ShapeDtypeStruct((rows, LANES), BF16),
        ),
        in_specs=[vmem],
        out_specs=(vmem,) * 5,
        name="edges",
    )(u)

    up = [(i, i + 1) for i in range(count - 1)]
    down = [(i + 1, i) for i in range(count - 1)]
    span_up = [(i, i + 1) for i in range(spans - 1)]
    span_down = [(i + 1, i) for i in range(spans - 1)]
    rim_two = jnp.concatenate([rim, lax.ppermute(rim, "stream", around(count, 1))], 0)
    far = [
        lax.ppermute(rim_two, "stream", around(count, count // 2 + offset))
        for offset in range(-REACH, OWNERS - REACH, 2)
    ]
    from_west = lax.ppermute(east, "stream", up)
    from_east = lax.ppermute(west, "stream", down)
    from_south = lax.ppermute(north, "span", span_up)
    from_north = lax.ppermute(south, "span", span_down)

    live = tile_live.reshape(1)
    place = lax.axis_index("stream").astype(jnp.int32).reshape(1)
    trio = 3 * LANES
    rim_rows = 2 * cz + 2 * rows
    work, green, shift, pick, rim_weights = pl.pallas_call(
        functools.partial(local_kernel, (times, cx, cz, pairs, points, count)),
        out_shape=(
            jax.ShapeDtypeStruct((lines, width), F32),
            jax.ShapeDtypeStruct((pairs, 4, wide, wide), BF16),
            jax.ShapeDtypeStruct((2 * LANES, LANES), BF16),
            jax.ShapeDtypeStruct((rows, OWNERS * rows), BF16),
            jax.ShapeDtypeStruct((rim_rows, trio), F32),
        ),
        grid=(pairs,),
        in_specs=[
            smem,
            smem,
            smem,
            smem,
            pl.BlockSpec((lines, trio), lambda p: (0, p)),
            pl.BlockSpec((times, cx, cz, trio), lambda p: (0, 0, 0, p)),
            pl.BlockSpec((rows, 4 * points), lambda p: (0, 0)),
            pl.BlockSpec((states, points), lambda p: (0, 0)),
            pl.BlockSpec((states, points), lambda p: (0, 0)),
            pl.BlockSpec((rows, 1), lambda p: (0, 0)),
            pl.BlockSpec((1, rows), lambda p: (0, 0)),
        ],
        out_specs=(
            pl.BlockSpec((lines, trio), lambda p: (0, p)),
            pl.BlockSpec((1, 4, wide, wide), lambda p: (p, 0, 0, 0)),
            pl.BlockSpec((2 * LANES, LANES), lambda p: (0, 0)),
            pl.BlockSpec((rows, OWNERS * rows), lambda p: (0, 0)),
            pl.BlockSpec((rim_rows, trio), lambda p: (0, 0)),
        ),
        scratch_shapes=[
            pltpu.VMEM((8, wide), F32),
            pltpu.VMEM((8, wide), F32),
            pltpu.VMEM((8, wide), F32),
            pltpu.VMEM((8, wide), F32),
            pltpu.VMEM((wide, 8), F32),
            pltpu.VMEM((wide, 8), F32),
            pltpu.VMEM((4 * rows, trio), F32),
            pltpu.VMEM((lines, trio), F32),
        ],
        compiler_params=pltpu.CompilerParams(vmem_limit_bytes=48 * 2**20),
        cost_estimate=pl.CostEstimate(flops=20_000_000, bytes_accessed=6_000_000, transcendentals=400_000),
        name="local",
    )(
        omega,
        phase,
        live,
        place,
        u,
        source,
        stencil.reshape(rows, 4 * points),
        line_coupling,
        line_diag,
        match_owner.reshape(rows, 1),
        match_row.reshape(1, rows),
    )

    whole = lambda array: pl.BlockSpec(array.shape, lambda p: (0, 0))
    edge = lambda array: pl.BlockSpec((array.shape[0], trio), lambda p: (0, p))
    updated = pl.pallas_call(
        functools.partial(finish_kernel, (times, cx, cz, pairs, points), len(far)),
        out_shape=jax.ShapeDtypeStruct((lines, width), F32),
        grid=(pairs,),
        in_specs=[smem]
        + [whole(piece) for piece in far]
        + [
            edge(work),
            pl.BlockSpec((1, 4, wide, wide), lambda p: (p, 0, 0, 0)),
            whole(shift),
            whole(pick),
            whole(rim_weights),
            edge(from_west),
            edge(from_east),
            edge(from_south),
            edge(from_north),
        ],
        out_specs=edge(work),
        scratch_shapes=[
            pltpu.VMEM((OWNERS * rows, LANES), BF16),
            pltpu.VMEM((rows, LANES), F32),
            pltpu.VMEM((cx * 8, trio), F32),
            pltpu.VMEM((cx * 8, trio), F32),
            pltpu.VMEM((2, lines, wide), BF16),
            pltpu.VMEM((2, lines, wide), BF16),
        ],
        compiler_params=pltpu.CompilerParams(vmem_limit_bytes=48 * 2**20),
        cost_estimate=pl.CostEstimate(flops=800_000_000, bytes_accessed=5_000_000, transcendentals=0),
        name="finish",
    )(live, *far, work, green, shift, pick, rim_weights, from_west, from_east, from_south, from_north)
    return updated.reshape(times, cx, cz, width)


def solution(mesh):
    in_specs = (
        P(None, "stream", "span", None),
        P(None, "stream", "span", None),
        P("stream", "span", None),
        P(),
        P(),
        P(),
        P(),
        P("stream", "span", None, None),
        P("stream", "span", None),
        P("stream", "span"),
    )
    out_specs = P(None, "stream", "span", None)
    return jax.shard_map(body, mesh=mesh, in_specs=in_specs, out_specs=out_specs, check_vma=False)
```

```python
import functools
import math

import jax
import jax.numpy as jnp
from jax import lax
from jax.experimental import pallas as pl
from jax.experimental.pallas import tpu as pltpu
from jax.sharding import PartitionSpec as P

F32 = jnp.float32
BF16 = jnp.bfloat16
LANES = 128
HALF = 64
REACH = 3
OWNERS = 8
VMEM_GRANT = 60 * 2**20
GROUPS = 3
PARTS = 1


def iota(shape, dim):
    return lax.broadcasted_iota(jnp.int32, shape, dim)


def split(value):
    high = value.astype(BF16)
    return high, (value - high.astype(F32)).astype(BF16)


def edge_kernel(dims, u_ref, first_x_ref, second_x_ref, first_z_ref, second_z_ref, rim_ref):
    times, cx, cz, pairs = dims
    rows = cx * cz
    width = u_ref.shape[1]
    lane = iota((rows, LANES), 1)
    inner = lane % HALF
    span = times * pairs
    found = jnp.zeros((rows, LANES), F32)
    for t in range(times):
        for pair in range(pairs):
            base = pair * 3 * LANES
            block = slice(t * rows, (t + 1) * rows)
            first = u_ref[block, base + LANES : base + 2 * LANES]
            second = u_ref[block, base + 2 * LANES : base + 3 * LANES]
            both = jnp.where(lane < HALF, first, second)
            spot = t * pairs + pair
            both = pltpu.roll(both, (spot - (HALF - 1)) % LANES, 1)
            found = jnp.where(inner == spot, both, found)
    part = rows // GROUPS
    parts = []
    for _ in range(PARTS):
        rounded = found.astype(BF16).astype(F32)
        found = found - rounded
        packed = rounded[:part]
        for group in range(1, GROUPS):
            packed = packed + pltpu.roll(rounded[group * part : (group + 1) * part], group * span, 1)
        parts.append(packed)
    packed = jnp.concatenate(parts, 0).astype(BF16)
    for other in range(rim_ref.shape[0]):
        rim_ref[other] = packed

    take = lambda t, x: u_ref[t * rows + x * cz : t * rows + x * cz + cz, :]
    west = jnp.concatenate([take(t, 0) for t in range(times)], 0)
    east = jnp.concatenate([take(t, cx - 1) for t in range(times)], 0)
    even_x = lax.axis_index("stream") % 2 == 0
    first_x_ref[...] = jnp.where(even_x, east, west).astype(BF16)
    second_x_ref[...] = jnp.where(even_x, west, east).astype(BF16)
    sub = iota((8, width), 0)
    even_z = lax.axis_index("span") % 2 == 0
    top = cz - 1
    for ref, z in ((first_z_ref, jnp.where(even_z, top, 0)), (second_z_ref, jnp.where(even_z, 0, top))):
        tiles = []
        for x in range(cx):
            tile = jnp.zeros((8, width), F32)
            for t in range(times):
                tile = jnp.where(sub == t, u_ref[pl.ds(t * rows + x * cz + z, 1), :], tile)
            tiles.append(tile)
        ref[...] = jnp.concatenate(tiles, 0).astype(BF16)


def scan_products(matrix, lane, points, backward):
    a, b, c, d = matrix
    step = 1
    while step < points:
        shift = (lane.shape[1] - step) if backward else step
        inside = (lane < points - step) if backward else (lane >= step)
        e = jnp.where(inside, pltpu.roll(a, shift, 1), 1.0)
        f = jnp.where(inside, pltpu.roll(b, shift, 1), 0.0)
        g = jnp.where(inside, pltpu.roll(c, shift, 1), 0.0)
        h = jnp.where(inside, pltpu.roll(d, shift, 1), 1.0)
        a, b, c, d = a * e + b * g, a * f + b * h, c * e + d * g, c * f + d * h
        scale = 1.0 / (a + b + c + d)
        a, b, c, d = a * scale, b * scale, c * scale, d * scale
        step *= 2
    return a / c


def local_kernel(
    dims,
    omega_ref,
    phase_ref,
    live_ref,
    u_ref,
    source_ref,
    stencil_ref,
    coupling_ref,
    diag_ref,
    owner_ref,
    row_ref,
    work_ref,
    green_ref,
    shift_ref,
    pick_ref,
    keep_ref,
    rimw_ref,
    couple_s,
    diag_s,
    green_row,
    sum_row,
    green_col,
    sum_col,
    face_s,
    round_s,
):
    times, cx, cz, pairs, points, count = dims
    rows = cx * cz
    span = times * pairs
    pair_now = pl.program_id(0)
    wide = couple_s.shape[1]

    @pl.when(pair_now == 0)
    def prepare():
        states = coupling_ref.shape[0]
        lane = iota((8, wide), 1)
        couple_s[...] = jnp.ones_like(couple_s)
        diag_s[...] = jnp.ones_like(diag_s)
        couple_s[0:states, 0:points] = coupling_ref[...]
        diag_s[0:states, 0:points] = diag_ref[...]
        link = couple_s[...]
        diag = diag_s[...]
        before = jnp.where(lane == 0, 0.0, pltpu.roll(link, 1, 1))
        one = jnp.ones_like(link)
        e = scan_products((diag + before, diag * before, one, before), lane, points, False)
        inside = lane < points
        matrix = (
            jnp.where(inside, diag + link, 1.0),
            jnp.where(inside, diag * link, 0.0),
            jnp.where(inside, one, 0.0),
            jnp.where(inside, link, 1.0),
        )
        f = jnp.where(inside, scan_products(matrix, lane, points, True), 1.0)
        e_before = jnp.where(lane == 0, 1.0, pltpu.roll(e, 1, 1))
        e_before = jnp.where(inside, e_before, 1.0)
        green = 1.0 / (before * e_before / (before + e_before) + f)
        decay = jnp.log(1.0 + f / jnp.where(lane == 0, 1.0, before))
        decay = jnp.where((lane == 0) | (lane >= points), 0.0, decay)
        step = 1
        while step < points:
            decay = decay + jnp.where(lane >= step, pltpu.roll(decay, step, 1), 0.0)
            step *= 2
        odd = iota((8, wide), 0) % 2 == 1
        green = jnp.where(odd, pltpu.roll(green, HALF, 1), green)
        decay = jnp.where(odd, pltpu.roll(decay, HALF, 1), decay)
        green_row[...] = green
        sum_row[...] = decay
        green_col[...] = green.T
        sum_col[...] = decay.T

        low = iota((rows, LANES), 1) < HALF
        z = iota((rows, 3 * LANES), 0) % cz
        for way in range(4):
            at = way // 2 * 3 * LANES
            t0, t1, t2 = (stencil_ref[:, at + k * LANES : at + (k + 1) * LANES] for k in range(3))
            if way % 2 == 0:
                swap = pltpu.roll(t0, HALF, 1)
                tiles = (t0, jnp.where(low, t1, swap), jnp.where(low, swap, pltpu.roll(t1, HALF, 1)))
            else:
                swap = pltpu.roll(t2, HALF, 1)
                other = pltpu.roll(t1, HALF, 1)
                tiles = (jnp.where(low, other, swap), jnp.where(low, swap, t1), t2)
            face = jnp.concatenate(tiles, 1)
            if way == 0:
                rimw_ref[0:cz, :] = face[0:cz]
            elif way == 1:
                rimw_ref[cz : 2 * cz, :] = face[rows - cz :]
            elif way == 2:
                rimw_ref[2 * cz : 2 * cz + rows, :] = jnp.where(z == 0, face, 0.0)
                face = jnp.where(z == 0, 0.0, face)
            else:
                rimw_ref[2 * cz + rows : 2 * cz + 2 * rows, :] = jnp.where(z == cz - 1, face, 0.0)
                face = jnp.where(z == cz - 1, 0.0, face)
            face_s[way * rows : (way + 1) * rows, :] = face

        slot = owner_ref[...] - lax.axis_index("stream") + (count // 2 + REACH)
        slot = jnp.where(slot < 0, slot + count, slot)
        slot = jnp.where(slot >= count, slot - count, slot)
        diagonal = iota((rows, rows), 0) == iota((rows, rows), 1)
        target = jnp.sum(jnp.where(diagonal, row_ref[...].astype(F32), 0.0), axis=1, keepdims=True)
        target = target.astype(jnp.int32)
        part = rows // GROUPS
        group = jnp.zeros_like(target)
        for k in range(1, GROUPS):
            group = group + jnp.where(target >= k * part, 1, 0)
        wanted = slot * part + target - group * part
        cell = iota((rows, OWNERS * part), 1)
        pick_ref[...] = jnp.where(cell == wanted, 1.0, 0.0).astype(BF16)
        keep_ref[...] = jnp.where(iota((rows, LANES), 1) % HALF // span == group, 1.0, 0.0)

        left = iota((LANES, LANES), 0)
        right = iota((LANES, LANES), 1)
        left_in = left % HALF
        right_in = right % HALF
        left_in_part = left_in % span
        offset = right_in // pairs - left_in_part // pairs
        angle = (2.0 * math.pi / times) * offset.astype(F32)
        total = jnp.ones((LANES, LANES), F32)
        for harmonic in range(1, (times - 1) // 2 + 1):
            total = total + 2.0 * jnp.cos(harmonic * (angle + phase_ref[0]))
        ok = (left // HALF != right // HALF) & (left_in_part % pairs == right_in % pairs)
        ok = ok & (right_in < span) & (left_in < 3 * span)
        high, low_part = split(jnp.where(ok, total / times, 0.0))
        shift_ref[0:LANES, :] = high
        shift_ref[LANES : 2 * LANES, :] = low_part

    for half in range(2):
        state = 2 * pair_now + half
        first = half * HALF
        g_row = green_row[pl.ds(state, 1), :]
        s_row = sum_row[pl.ds(state, 1), :]
        pick = iota((wide, 8), 1) == state
        g_col = jnp.sum(jnp.where(pick, green_col[...], 0.0), axis=1, keepdims=True)
        s_col = jnp.sum(jnp.where(pick, sum_col[...], 0.0), axis=1, keepdims=True)
        k = iota((wide, wide), 0)
        n = iota((wide, wide), 1)
        full = jnp.exp(-jnp.abs(s_col - s_row)) * jnp.where(k <= n, g_col, g_row)
        at_end = first + points - 1
        lane = iota((1, wide), 1)
        s_end = jnp.sum(jnp.where(lane == at_end, s_row, 0.0), axis=1, keepdims=True)
        link = couple_s[pl.ds(state, 1), :]
        c_end = jnp.sum(jnp.where(lane == points - 1, link, 0.0), axis=1, keepdims=True)
        last = c_end * jnp.exp(-jnp.abs(s_end - s_row)) * g_row
        inside_k = (k >= first) & (k < first + points)
        inside_n = (n >= first) & (n < first + points)
        inner = k % HALF
        added = (inner < span) & (inner % pairs == pair_now)
        full = jnp.where(inside_k, full, jnp.where(added, last, 0.0))
        full = jnp.where(inside_n, full, 0.0)
        high, low_part = split(full)
        green_ref[0, 2 * half] = high
        green_ref[0, 2 * half + 1] = low_part

    round_s[...] = u_ref[...].astype(BF16).astype(F32)
    omega = omega_ref[0]
    live = live_ref[0]
    z = iota((cz, 3 * LANES), 0)
    weights = []
    for n in range(1, (times - 1) // 2 + 1):
        weights.append(omega * (0.5 * (-1.0) ** n / math.sin(math.pi * n / times)))
    for x in range(cx):
        west, east, south, north = (
            face_s[way * rows + x * cz : way * rows + (x + 1) * cz, :] for way in range(4)
        )
        for t in range(times):
            at = lambda tt, xx: slice((tt % times) * rows + xx * cz, (tt % times) * rows + (xx + 1) * cz)
            here = round_s[at(t, x), :]
            value = source_ref[t, x].astype(F32)
            value += south * pltpu.roll(here, 1, 0) + north * pltpu.roll(here, cz - 1, 0)
            if x > 0:
                value += west * round_s[at(t, x - 1), :]
            if x < cx - 1:
                value += east * round_s[at(t, x + 1), :]
            for n, weight in enumerate(weights, 1):
                value -= weight * (u_ref[at(t + n, x), :] - u_ref[at(t - n, x), :])
            work_ref[at(t, x), :] = jnp.where(z + x * cz < live, value, u_ref[at(t, x), :])


def finish_kernel(
    dims,
    live_ref,
    rim_ref,
    work_ref,
    green_ref,
    shift_ref,
    pick_ref,
    keep_ref,
    rimw_ref,
    first_x_ref,
    second_x_ref,
    first_z_ref,
    second_z_ref,
    out_ref,
    rim_s,
    ghost_s,
    south_s,
    north_s,
    high_s,
    low_s,
):
    times, cx, cz, pairs, points, count = dims
    rows = cx * cz
    part = rows // GROUPS

    @pl.when(pl.program_id(0) == 0)
    def ghosts():
        ghost = jnp.zeros((rows, LANES), F32)
        for piece in range(PARTS):
            for k in range(OWNERS):
                owner = lax.rem(lax.axis_index("stream") + (count + count // 2 - REACH + k), count)
                rim_s[k * part : (k + 1) * part, :] = rim_ref[owner, piece * part : (piece + 1) * part]
            picked = jnp.dot(pick_ref[...], rim_s[...], preferred_element_type=F32)
            picked = (picked * keep_ref[...]).astype(BF16)
            ghost += jnp.dot(picked, shift_ref[0:LANES, :], preferred_element_type=F32)
            ghost += jnp.dot(picked, shift_ref[LANES : 2 * LANES, :], preferred_element_type=F32)
        ghost_s[...] = ghost

    first = first_x_ref[...].astype(F32)
    second = second_x_ref[...].astype(F32)
    even_x = lax.axis_index("stream") % 2 == 0
    west = jnp.where(even_x, second, first)
    east = jnp.where(even_x, first, second)
    first = first_z_ref[...].astype(F32)
    second = second_z_ref[...].astype(F32)
    even_z = lax.axis_index("span") % 2 == 0
    south_s[...] = jnp.where(even_z, second, first)
    north_s[...] = jnp.where(even_z, first, second)
    lane = iota((cz, LANES), 1)
    inner = lane % HALF
    low_half = lane < HALF
    for t in range(times):
        mine = (inner >= t * pairs) & (inner < (t + 1) * pairs)
        even, odd = [], []
        for x in range(cx):
            at = t * rows + x * cz
            value = work_ref[at : at + cz, :]
            if x == 0:
                value += rimw_ref[0:cz, :] * west[t * cz : (t + 1) * cz]
            if x == cx - 1:
                value += rimw_ref[cz : 2 * cz, :] * east[t * cz : (t + 1) * cz]
            south = rimw_ref[2 * cz + x * cz : 2 * cz + (x + 1) * cz, :]
            north = rimw_ref[2 * cz + rows + x * cz : 2 * cz + rows + (x + 1) * cz, :]
            value += south * south_s[x * 8 + t : x * 8 + t + 1, :]
            value += north * north_s[x * 8 + t : x * 8 + t + 1, :]
            ghost = jnp.where(mine, ghost_s[x * cz : (x + 1) * cz, :], 0.0)
            mid = value[:, LANES : 2 * LANES]
            even.append(jnp.concatenate([value[:, :LANES], jnp.where(low_half, mid, ghost)], 1))
            odd.append(jnp.concatenate([jnp.where(low_half, ghost, mid), value[:, 2 * LANES :]], 1))
        for half, pieces in ((0, even), (1, odd)):
            high, low = split(jnp.concatenate(pieces, 0))
            high_s[half, t * rows : (t + 1) * rows, :] = high
            low_s[half, t * rows : (t + 1) * rows, :] = low
    products = []
    for half in range(2):
        high = high_s[half]
        g_high = green_ref[0, 2 * half]
        total = jnp.dot(high, g_high, preferred_element_type=F32)
        total += jnp.dot(high, green_ref[0, 2 * half + 1], preferred_element_type=F32)
        total += jnp.dot(low_s[half], g_high, preferred_element_type=F32)
        products.append(total)
    even, odd = products
    tiles = (even[:, :LANES], even[:, LANES:] + odd[:, :LANES], odd[:, LANES:])
    live = live_ref[0]
    shape = out_ref.shape[:1] + (LANES,)
    alive = iota(shape, 0) % rows < live
    for k, tile in enumerate(tiles):
        lanes = slice(k * LANES, (k + 1) * LANES)
        out_ref[:, lanes] = jnp.where(alive, tile, work_ref[:, lanes])


def pairing(count, first):
    up = [(i, i + 1) for i in range(first, count - 1, 2)]
    return up + [(b, a) for a, b in up]


def body(
    adjoint,
    source,
    stencil,
    line_coupling,
    line_diag,
    omega,
    phase,
    match_owner,
    match_row,
    tile_live,
):
    times, cx, cz, width = adjoint.shape
    states, points = line_coupling.shape
    pairs = states // 2
    rows = cx * cz
    lines = times * rows
    count = lax.axis_size("stream")
    spans = lax.axis_size("span")
    wide = 2 * LANES
    u = adjoint.reshape(lines, width)
    vmem = pl.BlockSpec(memory_space=pltpu.VMEM)
    smem = pl.BlockSpec(memory_space=pltpu.SMEM)
    part = rows // GROUPS
    first_x, second_x, first_z, second_z, rim = pl.pallas_call(
        functools.partial(edge_kernel, (times, cx, cz, pairs)),
        out_shape=(
            jax.ShapeDtypeStruct((times * cz, width), BF16),
            jax.ShapeDtypeStruct((times * cz, width), BF16),
            jax.ShapeDtypeStruct((cx * 8, width), BF16),
            jax.ShapeDtypeStruct((cx * 8, width), BF16),
            jax.ShapeDtypeStruct((count, PARTS * part, LANES), BF16),
        ),
        in_specs=[vmem],
        out_specs=(vmem,) * 5,
        compiler_params=pltpu.CompilerParams(vmem_limit_bytes=VMEM_GRANT),
        name="edges",
    )(u)

    rims = lax.all_to_all(rim, "stream", 0, 0)
    first_x = lax.ppermute(first_x, "stream", pairing(count, 0))
    second_z, second_x, _ = lax.optimization_barrier((second_z, second_x, first_x))
    second_z = lax.ppermute(second_z, "span", pairing(spans, 1))
    second_x = lax.ppermute(second_x, "stream", pairing(count, 1))
    first_z = lax.ppermute(first_z, "span", pairing(spans, 0))

    live = tile_live.reshape(1)
    trio = 3 * LANES
    rim_rows = 2 * cz + 2 * rows
    work, green, shift, pick, keep, rim_weights = pl.pallas_call(
        functools.partial(local_kernel, (times, cx, cz, pairs, points, count)),
        out_shape=(
            jax.ShapeDtypeStruct((lines, width), F32),
            jax.ShapeDtypeStruct((pairs, 4, wide, wide), BF16),
            jax.ShapeDtypeStruct((2 * LANES, LANES), BF16),
            jax.ShapeDtypeStruct((rows, OWNERS * part), BF16),
            jax.ShapeDtypeStruct((rows, LANES), F32),
            jax.ShapeDtypeStruct((rim_rows, trio), F32),
        ),
        grid=(pairs,),
        in_specs=[
            smem,
            smem,
            smem,
            pl.BlockSpec((lines, trio), lambda p: (0, p)),
            pl.BlockSpec((times, cx, cz, trio), lambda p: (0, 0, 0, p)),
            pl.BlockSpec((rows, 4 * points), lambda p: (0, 0)),
            pl.BlockSpec((states, points), lambda p: (0, 0)),
            pl.BlockSpec((states, points), lambda p: (0, 0)),
            pl.BlockSpec((rows, 1), lambda p: (0, 0)),
            pl.BlockSpec((1, rows), lambda p: (0, 0)),
        ],
        out_specs=(
            pl.BlockSpec((lines, trio), lambda p: (0, p)),
            pl.BlockSpec((1, 4, wide, wide), lambda p: (p, 0, 0, 0)),
            pl.BlockSpec((2 * LANES, LANES), lambda p: (0, 0)),
            pl.BlockSpec((rows, OWNERS * part), lambda p: (0, 0)),
            pl.BlockSpec((rows, LANES), lambda p: (0, 0)),
            pl.BlockSpec((rim_rows, trio), lambda p: (0, 0)),
        ),
        scratch_shapes=[
            pltpu.VMEM((8, wide), F32),
            pltpu.VMEM((8, wide), F32),
            pltpu.VMEM((8, wide), F32),
            pltpu.VMEM((8, wide), F32),
            pltpu.VMEM((wide, 8), F32),
            pltpu.VMEM((wide, 8), F32),
            pltpu.VMEM((4 * rows, trio), F32),
            pltpu.VMEM((lines, trio), F32),
        ],
        compiler_params=pltpu.CompilerParams(vmem_limit_bytes=VMEM_GRANT),
        cost_estimate=pl.CostEstimate(flops=20_000_000, bytes_accessed=6_000_000, transcendentals=400_000),
        name="local",
    )(
        omega,
        phase,
        live,
        u,
        source,
        stencil.reshape(rows, 4 * points),
        line_coupling,
        line_diag,
        match_owner.reshape(rows, 1),
        match_row.reshape(1, rows),
    )

    whole = lambda array: pl.BlockSpec(array.shape, lambda p: (0, 0))
    edge = lambda array: pl.BlockSpec((array.shape[0], trio), lambda p: (0, p))
    updated = pl.pallas_call(
        functools.partial(finish_kernel, (times, cx, cz, pairs, points, count)),
        out_shape=jax.ShapeDtypeStruct((lines, width), F32),
        grid=(pairs,),
        in_specs=[
            smem,
            pl.BlockSpec(rims.shape, lambda p: (0, 0, 0)),
            edge(work),
            pl.BlockSpec((1, 4, wide, wide), lambda p: (p, 0, 0, 0)),
            whole(shift),
            whole(pick),
            whole(keep),
            whole(rim_weights),
            edge(first_x),
            edge(second_x),
            edge(first_z),
            edge(second_z),
        ],
        out_specs=edge(work),
        scratch_shapes=[
            pltpu.VMEM((OWNERS * part, LANES), BF16),
            pltpu.VMEM((rows, LANES), F32),
            pltpu.VMEM((cx * 8, trio), F32),
            pltpu.VMEM((cx * 8, trio), F32),
            pltpu.VMEM((2, lines, wide), BF16),
            pltpu.VMEM((2, lines, wide), BF16),
        ],
        compiler_params=pltpu.CompilerParams(vmem_limit_bytes=VMEM_GRANT),
        cost_estimate=pl.CostEstimate(flops=800_000_000, bytes_accessed=5_000_000, transcendentals=0),
        name="finish",
    )(
        live,
        rims,
        work,
        green,
        shift,
        pick,
        keep,
        rim_weights,
        first_x,
        second_x,
        first_z,
        second_z,
    )
    return updated.reshape(times, cx, cz, width)


def solution(mesh):
    in_specs = (
        P(None, "stream", "span", None),
        P(None, "stream", "span", None),
        P("stream", "span", None),
        P(),
        P(),
        P(),
        P(),
        P("stream", "span", None, None),
        P("stream", "span", None),
        P("stream", "span"),
    )
    out_specs = P(None, "stream", "span", None)
    return jax.shard_map(body, mesh=mesh, in_specs=in_specs, out_specs=out_specs, check_vma=False)
```

```python
import functools
import math

import jax
import jax.numpy as jnp
from jax import lax
from jax.experimental import pallas as pl
from jax.experimental.pallas import tpu as pltpu
from jax.sharding import PartitionSpec as P

F32 = jnp.float32
BF16 = jnp.bfloat16
LANES = 128
HALF = 64
REACH = 3
OWNERS = 8
VMEM_GRANT = 60 * 2**20
GROUPS = 3
PARTS = 1


def iota(shape, dim):
    return lax.broadcasted_iota(jnp.int32, shape, dim)


def split(value):
    high = value.astype(BF16)
    return high, (value - high.astype(F32)).astype(BF16)


def edge_kernel(dims, u_ref, rim_ref, second_z_ref, second_x_ref, first_z_ref, first_x_ref):
    times, cx, cz, pairs = dims
    rows = cx * cz
    width = u_ref.shape[1]
    lane = iota((rows, LANES), 1)
    inner = lane % HALF
    span = times * pairs
    found = jnp.zeros((rows, LANES), F32)
    for t in range(times):
        for pair in range(pairs):
            base = pair * 3 * LANES
            block = slice(t * rows, (t + 1) * rows)
            first = u_ref[block, base + LANES : base + 2 * LANES]
            second = u_ref[block, base + 2 * LANES : base + 3 * LANES]
            both = jnp.where(lane < HALF, first, second)
            spot = t * pairs + pair
            both = pltpu.roll(both, (spot - (HALF - 1)) % LANES, 1)
            found = jnp.where(inner == spot, both, found)
    part = rows // GROUPS
    parts = []
    for _ in range(PARTS):
        rounded = found.astype(BF16).astype(F32)
        found = found - rounded
        packed = rounded[:part]
        for group in range(1, GROUPS):
            packed = packed + pltpu.roll(rounded[group * part : (group + 1) * part], group * span, 1)
        parts.append(packed)
    packed = jnp.concatenate(parts, 0).astype(BF16)
    for other in range(rim_ref.shape[0]):
        rim_ref[other] = packed

    take = lambda t, x: u_ref[t * rows + x * cz : t * rows + x * cz + cz, :]
    west = jnp.concatenate([take(t, 0) for t in range(times)], 0)
    east = jnp.concatenate([take(t, cx - 1) for t in range(times)], 0)
    even_x = lax.axis_index("stream") % 2 == 0
    first_x_ref[...] = jnp.where(even_x, east, west).astype(BF16)
    second_x_ref[...] = jnp.where(even_x, west, east).astype(BF16)
    sub = iota((8, width), 0)
    even_z = lax.axis_index("span") % 2 == 0
    top = cz - 1
    for ref, z in ((first_z_ref, jnp.where(even_z, top, 0)), (second_z_ref, jnp.where(even_z, 0, top))):
        tiles = []
        for x in range(cx):
            tile = jnp.zeros((8, width), F32)
            for t in range(times):
                tile = jnp.where(sub == t, u_ref[pl.ds(t * rows + x * cz + z, 1), :], tile)
            tiles.append(tile)
        ref[...] = jnp.concatenate(tiles, 0).astype(BF16)


def scan_products(matrix, lane, points, backward):
    a, b, c, d = matrix
    step = 1
    while step < points:
        shift = (lane.shape[1] - step) if backward else step
        inside = (lane < points - step) if backward else (lane >= step)
        e = jnp.where(inside, pltpu.roll(a, shift, 1), 1.0)
        f = jnp.where(inside, pltpu.roll(b, shift, 1), 0.0)
        g = jnp.where(inside, pltpu.roll(c, shift, 1), 0.0)
        h = jnp.where(inside, pltpu.roll(d, shift, 1), 1.0)
        a, b, c, d = a * e + b * g, a * f + b * h, c * e + d * g, c * f + d * h
        scale = 1.0 / (a + b + c + d)
        a, b, c, d = a * scale, b * scale, c * scale, d * scale
        step *= 2
    return a / c


def local_kernel(
    dims,
    omega_ref,
    phase_ref,
    live_ref,
    u_ref,
    source_ref,
    stencil_ref,
    coupling_ref,
    diag_ref,
    owner_ref,
    row_ref,
    work_ref,
    green_ref,
    shift_ref,
    pick_ref,
    keep_ref,
    rimw_ref,
    couple_s,
    diag_s,
    green_row,
    sum_row,
    green_col,
    sum_col,
    face_s,
    round_s,
):
    times, cx, cz, pairs, points, count = dims
    rows = cx * cz
    span = times * pairs
    pair_now = pl.program_id(0)
    wide = couple_s.shape[1]

    @pl.when(pair_now == 0)
    def prepare():
        states = coupling_ref.shape[0]
        lane = iota((8, wide), 1)
        couple_s[...] = jnp.ones_like(couple_s)
        diag_s[...] = jnp.ones_like(diag_s)
        couple_s[0:states, 0:points] = coupling_ref[...]
        diag_s[0:states, 0:points] = diag_ref[...]
        link = couple_s[...]
        diag = diag_s[...]
        before = jnp.where(lane == 0, 0.0, pltpu.roll(link, 1, 1))
        one = jnp.ones_like(link)
        e = scan_products((diag + before, diag * before, one, before), lane, points, False)
        inside = lane < points
        matrix = (
            jnp.where(inside, diag + link, 1.0),
            jnp.where(inside, diag * link, 0.0),
            jnp.where(inside, one, 0.0),
            jnp.where(inside, link, 1.0),
        )
        f = jnp.where(inside, scan_products(matrix, lane, points, True), 1.0)
        e_before = jnp.where(lane == 0, 1.0, pltpu.roll(e, 1, 1))
        e_before = jnp.where(inside, e_before, 1.0)
        green = 1.0 / (before * e_before / (before + e_before) + f)
        decay = jnp.log(1.0 + f / jnp.where(lane == 0, 1.0, before))
        decay = jnp.where((lane == 0) | (lane >= points), 0.0, decay)
        step = 1
        while step < points:
            decay = decay + jnp.where(lane >= step, pltpu.roll(decay, step, 1), 0.0)
            step *= 2
        odd = iota((8, wide), 0) % 2 == 1
        green = jnp.where(odd, pltpu.roll(green, HALF, 1), green)
        decay = jnp.where(odd, pltpu.roll(decay, HALF, 1), decay)
        green_row[...] = green
        sum_row[...] = decay
        green_col[...] = green.T
        sum_col[...] = decay.T

        low = iota((rows, LANES), 1) < HALF
        z = iota((rows, 3 * LANES), 0) % cz
        for way in range(4):
            at = way // 2 * 3 * LANES
            t0, t1, t2 = (stencil_ref[:, at + k * LANES : at + (k + 1) * LANES] for k in range(3))
            if way % 2 == 0:
                swap = pltpu.roll(t0, HALF, 1)
                tiles = (t0, jnp.where(low, t1, swap), jnp.where(low, swap, pltpu.roll(t1, HALF, 1)))
            else:
                swap = pltpu.roll(t2, HALF, 1)
                other = pltpu.roll(t1, HALF, 1)
                tiles = (jnp.where(low, other, swap), jnp.where(low, swap, t1), t2)
            face = jnp.concatenate(tiles, 1)
            if way == 0:
                rimw_ref[0:cz, :] = face[0:cz]
            elif way == 1:
                rimw_ref[cz : 2 * cz, :] = face[rows - cz :]
            elif way == 2:
                rimw_ref[2 * cz : 2 * cz + rows, :] = jnp.where(z == 0, face, 0.0)
                face = jnp.where(z == 0, 0.0, face)
            else:
                rimw_ref[2 * cz + rows : 2 * cz + 2 * rows, :] = jnp.where(z == cz - 1, face, 0.0)
                face = jnp.where(z == cz - 1, 0.0, face)
            face_s[way * rows : (way + 1) * rows, :] = face

        slot = owner_ref[...] - lax.axis_index("stream") + (count // 2 + REACH)
        slot = jnp.where(slot < 0, slot + count, slot)
        slot = jnp.where(slot >= count, slot - count, slot)
        diagonal = iota((rows, rows), 0) == iota((rows, rows), 1)
        target = jnp.sum(jnp.where(diagonal, row_ref[...].astype(F32), 0.0), axis=1, keepdims=True)
        target = target.astype(jnp.int32)
        part = rows // GROUPS
        group = jnp.zeros_like(target)
        for k in range(1, GROUPS):
            group = group + jnp.where(target >= k * part, 1, 0)
        wanted = slot * part + target - group * part
        cell = iota((rows, OWNERS * part), 1)
        pick_ref[...] = jnp.where(cell == wanted, 1.0, 0.0).astype(BF16)
        keep_ref[...] = jnp.where(iota((rows, LANES), 1) % HALF // span == group, 1.0, 0.0)

        left = iota((LANES, LANES), 0)
        right = iota((LANES, LANES), 1)
        left_in = left % HALF
        right_in = right % HALF
        left_in_part = left_in % span
        offset = right_in // pairs - left_in_part // pairs
        angle = (2.0 * math.pi / times) * offset.astype(F32)
        total = jnp.ones((LANES, LANES), F32)
        for harmonic in range(1, (times - 1) // 2 + 1):
            total = total + 2.0 * jnp.cos(harmonic * (angle + phase_ref[0]))
        ok = (left // HALF != right // HALF) & (left_in_part % pairs == right_in % pairs)
        ok = ok & (right_in < span) & (left_in < 3 * span)
        high, low_part = split(jnp.where(ok, total / times, 0.0))
        shift_ref[0:LANES, :] = high
        shift_ref[LANES : 2 * LANES, :] = low_part

    for half in range(2):
        state = 2 * pair_now + half
        first = half * HALF
        g_row = green_row[pl.ds(state, 1), :]
        s_row = sum_row[pl.ds(state, 1), :]
        pick = iota((wide, 8), 1) == state
        g_col = jnp.sum(jnp.where(pick, green_col[...], 0.0), axis=1, keepdims=True)
        s_col = jnp.sum(jnp.where(pick, sum_col[...], 0.0), axis=1, keepdims=True)
        k = iota((wide, wide), 0)
        n = iota((wide, wide), 1)
        full = jnp.exp(-jnp.abs(s_col - s_row)) * jnp.where(k <= n, g_col, g_row)
        at_end = first + points - 1
        lane = iota((1, wide), 1)
        s_end = jnp.sum(jnp.where(lane == at_end, s_row, 0.0), axis=1, keepdims=True)
        link = couple_s[pl.ds(state, 1), :]
        c_end = jnp.sum(jnp.where(lane == points - 1, link, 0.0), axis=1, keepdims=True)
        last = c_end * jnp.exp(-jnp.abs(s_end - s_row)) * g_row
        inside_k = (k >= first) & (k < first + points)
        inside_n = (n >= first) & (n < first + points)
        inner = k % HALF
        added = (inner < span) & (inner % pairs == pair_now)
        full = jnp.where(inside_k, full, jnp.where(added, last, 0.0))
        full = jnp.where(inside_n, full, 0.0)
        high, low_part = split(full)
        green_ref[0, 2 * half] = high
        green_ref[0, 2 * half + 1] = low_part

    round_s[...] = u_ref[...].astype(BF16).astype(F32)
    omega = omega_ref[0]
    live = live_ref[0]
    z = iota((cz, 3 * LANES), 0)
    weights = []
    for n in range(1, (times - 1) // 2 + 1):
        weights.append(omega * (0.5 * (-1.0) ** n / math.sin(math.pi * n / times)))
    for x in range(cx):
        west, east, south, north = (
            face_s[way * rows + x * cz : way * rows + (x + 1) * cz, :] for way in range(4)
        )
        for t in range(times):
            at = lambda tt, xx: slice((tt % times) * rows + xx * cz, (tt % times) * rows + (xx + 1) * cz)
            here = round_s[at(t, x), :]
            value = source_ref[t, x].astype(F32)
            value += south * pltpu.roll(here, 1, 0) + north * pltpu.roll(here, cz - 1, 0)
            if x > 0:
                value += west * round_s[at(t, x - 1), :]
            if x < cx - 1:
                value += east * round_s[at(t, x + 1), :]
            for n, weight in enumerate(weights, 1):
                value -= weight * (u_ref[at(t + n, x), :] - u_ref[at(t - n, x), :])
            work_ref[at(t, x), :] = jnp.where(z + x * cz < live, value, u_ref[at(t, x), :])


def finish_kernel(
    dims,
    live_ref,
    rim_ref,
    work_ref,
    green_ref,
    shift_ref,
    pick_ref,
    keep_ref,
    rimw_ref,
    second_z_ref,
    second_x_ref,
    first_z_ref,
    first_x_ref,
    out_ref,
    rim_s,
    ghost_s,
    south_s,
    north_s,
    high_s,
    low_s,
):
    times, cx, cz, pairs, points, count = dims
    rows = cx * cz
    part = rows // GROUPS

    @pl.when(pl.program_id(0) == 0)
    def ghosts():
        ghost = jnp.zeros((rows, LANES), F32)
        for piece in range(PARTS):
            for k in range(OWNERS):
                owner = lax.rem(lax.axis_index("stream") + (count + count // 2 - REACH + k), count)
                rim_s[k * part : (k + 1) * part, :] = rim_ref[owner, piece * part : (piece + 1) * part]
            picked = jnp.dot(pick_ref[...], rim_s[...], preferred_element_type=F32)
            picked = (picked * keep_ref[...]).astype(BF16)
            ghost += jnp.dot(picked, shift_ref[0:LANES, :], preferred_element_type=F32)
            ghost += jnp.dot(picked, shift_ref[LANES : 2 * LANES, :], preferred_element_type=F32)
        ghost_s[...] = ghost

    first = first_x_ref[...].astype(F32)
    second = second_x_ref[...].astype(F32)
    even_x = lax.axis_index("stream") % 2 == 0
    west = jnp.where(even_x, second, first)
    east = jnp.where(even_x, first, second)
    first = first_z_ref[...].astype(F32)
    second = second_z_ref[...].astype(F32)
    even_z = lax.axis_index("span") % 2 == 0
    south_s[...] = jnp.where(even_z, second, first)
    north_s[...] = jnp.where(even_z, first, second)
    lane = iota((cz, LANES), 1)
    inner = lane % HALF
    low_half = lane < HALF
    for t in range(times):
        mine = (inner >= t * pairs) & (inner < (t + 1) * pairs)
        even, odd = [], []
        for x in range(cx):
            at = t * rows + x * cz
            value = work_ref[at : at + cz, :]
            if x == 0:
                value += rimw_ref[0:cz, :] * west[t * cz : (t + 1) * cz]
            if x == cx - 1:
                value += rimw_ref[cz : 2 * cz, :] * east[t * cz : (t + 1) * cz]
            south = rimw_ref[2 * cz + x * cz : 2 * cz + (x + 1) * cz, :]
            north = rimw_ref[2 * cz + rows + x * cz : 2 * cz + rows + (x + 1) * cz, :]
            value += south * south_s[x * 8 + t : x * 8 + t + 1, :]
            value += north * north_s[x * 8 + t : x * 8 + t + 1, :]
            ghost = jnp.where(mine, ghost_s[x * cz : (x + 1) * cz, :], 0.0)
            mid = value[:, LANES : 2 * LANES]
            even.append(jnp.concatenate([value[:, :LANES], jnp.where(low_half, mid, ghost)], 1))
            odd.append(jnp.concatenate([jnp.where(low_half, ghost, mid), value[:, 2 * LANES :]], 1))
        for half, pieces in ((0, even), (1, odd)):
            high, low = split(jnp.concatenate(pieces, 0))
            high_s[half, t * rows : (t + 1) * rows, :] = high
            low_s[half, t * rows : (t + 1) * rows, :] = low
    products = []
    for half in range(2):
        high = high_s[half]
        g_high = green_ref[0, 2 * half]
        total = jnp.dot(high, g_high, preferred_element_type=F32)
        total += jnp.dot(high, green_ref[0, 2 * half + 1], preferred_element_type=F32)
        total += jnp.dot(low_s[half], g_high, preferred_element_type=F32)
        products.append(total)
    even, odd = products
    tiles = (even[:, :LANES], even[:, LANES:] + odd[:, :LANES], odd[:, LANES:])
    live = live_ref[0]
    shape = out_ref.shape[:1] + (LANES,)
    alive = iota(shape, 0) % rows < live
    for k, tile in enumerate(tiles):
        lanes = slice(k * LANES, (k + 1) * LANES)
        out_ref[:, lanes] = jnp.where(alive, tile, work_ref[:, lanes])


def pairing(count, first):
    up = [(i, i + 1) for i in range(first, count - 1, 2)]
    return up + [(b, a) for a, b in up]


def body(
    adjoint,
    source,
    stencil,
    line_coupling,
    line_diag,
    omega,
    phase,
    match_owner,
    match_row,
    tile_live,
):
    times, cx, cz, width = adjoint.shape
    states, points = line_coupling.shape
    pairs = states // 2
    rows = cx * cz
    lines = times * rows
    count = lax.axis_size("stream")
    spans = lax.axis_size("span")
    wide = 2 * LANES
    u = adjoint.reshape(lines, width)
    vmem = pl.BlockSpec(memory_space=pltpu.VMEM)
    smem = pl.BlockSpec(memory_space=pltpu.SMEM)
    part = rows // GROUPS
    rim, second_z, second_x, first_z, first_x = pl.pallas_call(
        functools.partial(edge_kernel, (times, cx, cz, pairs)),
        out_shape=(
            jax.ShapeDtypeStruct((count, PARTS * part, LANES), BF16),
            jax.ShapeDtypeStruct((cx * 8, width), BF16),
            jax.ShapeDtypeStruct((times * cz, width), BF16),
            jax.ShapeDtypeStruct((cx * 8, width), BF16),
            jax.ShapeDtypeStruct((times * cz, width), BF16),
        ),
        in_specs=[vmem],
        out_specs=(vmem,) * 5,
        compiler_params=pltpu.CompilerParams(vmem_limit_bytes=VMEM_GRANT),
        name="edges",
    )(u)

    rims = lax.all_to_all(rim, "stream", 0, 0)
    second_z = lax.ppermute(second_z, "span", pairing(spans, 1))
    second_x = lax.ppermute(second_x, "stream", pairing(count, 1))
    first_x = lax.ppermute(first_x, "stream", pairing(count, 0))
    first_z = lax.ppermute(first_z, "span", pairing(spans, 0))

    live = tile_live.reshape(1)
    trio = 3 * LANES
    rim_rows = 2 * cz + 2 * rows
    work, green, shift, pick, keep, rim_weights = pl.pallas_call(
        functools.partial(local_kernel, (times, cx, cz, pairs, points, count)),
        out_shape=(
            pltpu.HBM((lines, width), F32),
            pltpu.HBM((pairs, 4, wide, wide), BF16),
            pltpu.HBM((2 * LANES, LANES), BF16),
            pltpu.HBM((rows, OWNERS * part), BF16),
            pltpu.HBM((rows, LANES), F32),
            pltpu.HBM((rim_rows, trio), F32),
        ),
        grid=(pairs,),
        in_specs=[
            smem,
            smem,
            smem,
            pl.BlockSpec((lines, trio), lambda p: (0, p)),
            pl.BlockSpec((times, cx, cz, trio), lambda p: (0, 0, 0, p)),
            pl.BlockSpec((rows, 4 * points), lambda p: (0, 0)),
            pl.BlockSpec((states, points), lambda p: (0, 0)),
            pl.BlockSpec((states, points), lambda p: (0, 0)),
            pl.BlockSpec((rows, 1), lambda p: (0, 0)),
            pl.BlockSpec((1, rows), lambda p: (0, 0)),
        ],
        out_specs=(
            pl.BlockSpec((lines, trio), lambda p: (0, p)),
            pl.BlockSpec((1, 4, wide, wide), lambda p: (p, 0, 0, 0)),
            pl.BlockSpec((2 * LANES, LANES), lambda p: (0, 0)),
            pl.BlockSpec((rows, OWNERS * part), lambda p: (0, 0)),
            pl.BlockSpec((rows, LANES), lambda p: (0, 0)),
            pl.BlockSpec((rim_rows, trio), lambda p: (0, 0)),
        ),
        scratch_shapes=[
            pltpu.VMEM((8, wide), F32),
            pltpu.VMEM((8, wide), F32),
            pltpu.VMEM((8, wide), F32),
            pltpu.VMEM((8, wide), F32),
            pltpu.VMEM((wide, 8), F32),
            pltpu.VMEM((wide, 8), F32),
            pltpu.VMEM((4 * rows, trio), F32),
            pltpu.VMEM((lines, trio), F32),
        ],
        compiler_params=pltpu.CompilerParams(vmem_limit_bytes=16 * 2**20),
        cost_estimate=pl.CostEstimate(flops=20_000_000, bytes_accessed=6_000_000, transcendentals=400_000),
        name="local",
    )(
        omega,
        phase,
        live,
        u,
        source,
        stencil.reshape(rows, 4 * points),
        line_coupling,
        line_diag,
        match_owner.reshape(rows, 1),
        match_row.reshape(1, rows),
    )

    whole = lambda array: pl.BlockSpec(array.shape, lambda p: (0, 0))
    edge = lambda array: pl.BlockSpec((array.shape[0], trio), lambda p: (0, p))
    updated = pl.pallas_call(
        functools.partial(finish_kernel, (times, cx, cz, pairs, points, count)),
        out_shape=jax.ShapeDtypeStruct((lines, width), F32),
        grid=(pairs,),
        in_specs=[
            smem,
            pl.BlockSpec(rims.shape, lambda p: (0, 0, 0)),
            edge(work),
            pl.BlockSpec((1, 4, wide, wide), lambda p: (p, 0, 0, 0)),
            whole(shift),
            whole(pick),
            whole(keep),
            whole(rim_weights),
            edge(second_z),
            edge(second_x),
            edge(first_z),
            edge(first_x),
        ],
        out_specs=edge(work),
        scratch_shapes=[
            pltpu.VMEM((OWNERS * part, LANES), BF16),
            pltpu.VMEM((rows, LANES), F32),
            pltpu.VMEM((cx * 8, trio), F32),
            pltpu.VMEM((cx * 8, trio), F32),
            pltpu.VMEM((2, lines, wide), BF16),
            pltpu.VMEM((2, lines, wide), BF16),
        ],
        compiler_params=pltpu.CompilerParams(vmem_limit_bytes=65400 * 2**10),
        cost_estimate=pl.CostEstimate(flops=800_000_000, bytes_accessed=5_000_000, transcendentals=0),
        name="finish",
    )(
        live,
        rims,
        work,
        green,
        shift,
        pick,
        keep,
        rim_weights,
        second_z,
        second_x,
        first_z,
        first_x,
    )
    return updated.reshape(times, cx, cz, width)


def solution(mesh):
    in_specs = (
        P(None, "stream", "span", None),
        P(None, "stream", "span", None),
        P("stream", "span", None),
        P(),
        P(),
        P(),
        P(),
        P("stream", "span", None, None),
        P("stream", "span", None),
        P("stream", "span"),
    )
    out_specs = P(None, "stream", "span", None)
    return jax.shard_map(body, mesh=mesh, in_specs=in_specs, out_specs=out_specs, check_vma=False)
```

```python
import functools
import math

import jax
import jax.numpy as jnp
from jax import lax
from jax.experimental import pallas as pl
from jax.experimental.pallas import tpu as pltpu
from jax.sharding import PartitionSpec as P

F32 = jnp.float32
BF16 = jnp.bfloat16
LANES = 128
HALF = 64
REACH = 3
OWNERS = 8
VMEM_GRANT = 60 * 2**20
GROUPS = 3
PARTS = 1


def iota(shape, dim):
    return lax.broadcasted_iota(jnp.int32, shape, dim)


def split(value):
    high = value.astype(BF16)
    return high, (value - high.astype(F32)).astype(BF16)


def edge_kernel(dims, u_ref, rim_ref, second_z_ref, second_x_ref, first_z_ref, first_x_ref):
    times, cx, cz, pairs = dims
    rows = cx * cz
    width = u_ref.shape[1]
    lane = iota((rows, LANES), 1)
    inner = lane % HALF
    span = times * pairs
    found = jnp.zeros((rows, LANES), F32)
    for t in range(times):
        for pair in range(pairs):
            base = pair * 3 * LANES
            block = slice(t * rows, (t + 1) * rows)
            first = u_ref[block, base + LANES : base + 2 * LANES]
            second = u_ref[block, base + 2 * LANES : base + 3 * LANES]
            both = jnp.where(lane < HALF, first, second)
            spot = t * pairs + pair
            both = pltpu.roll(both, (spot - (HALF - 1)) % LANES, 1)
            found = jnp.where(inner == spot, both, found)
    part = rows // GROUPS
    parts = []
    for _ in range(PARTS):
        rounded = found.astype(BF16).astype(F32)
        found = found - rounded
        packed = rounded[:part]
        for group in range(1, GROUPS):
            packed = packed + pltpu.roll(rounded[group * part : (group + 1) * part], group * span, 1)
        parts.append(packed)
    packed = jnp.concatenate(parts, 0).astype(BF16)
    for other in range(rim_ref.shape[0]):
        rim_ref[other] = packed

    take = lambda t, x: u_ref[t * rows + x * cz : t * rows + x * cz + cz, :]
    west = jnp.concatenate([take(t, 0) for t in range(times)], 0)
    east = jnp.concatenate([take(t, cx - 1) for t in range(times)], 0)
    even_x = lax.axis_index("stream") % 2 == 0
    first_x_ref[...] = jnp.where(even_x, east, west).astype(BF16)
    second_x_ref[...] = jnp.where(even_x, west, east).astype(BF16)
    sub = iota((8, width), 0)
    even_z = lax.axis_index("span") % 2 == 0
    top = cz - 1
    for ref, z in ((first_z_ref, jnp.where(even_z, top, 0)), (second_z_ref, jnp.where(even_z, 0, top))):
        tiles = []
        for x in range(cx):
            tile = jnp.zeros((8, width), F32)
            for t in range(times):
                tile = jnp.where(sub == t, u_ref[pl.ds(t * rows + x * cz + z, 1), :], tile)
            tiles.append(tile)
        ref[...] = jnp.concatenate(tiles, 0).astype(BF16)


def scan_products(matrix, lane, points, backward):
    a, b, c, d = matrix
    step = 1
    while step < points:
        shift = (lane.shape[1] - step) if backward else step
        inside = (lane < points - step) if backward else (lane >= step)
        e = jnp.where(inside, pltpu.roll(a, shift, 1), 1.0)
        f = jnp.where(inside, pltpu.roll(b, shift, 1), 0.0)
        g = jnp.where(inside, pltpu.roll(c, shift, 1), 0.0)
        h = jnp.where(inside, pltpu.roll(d, shift, 1), 1.0)
        a, b, c, d = a * e + b * g, a * f + b * h, c * e + d * g, c * f + d * h
        scale = 1.0 / (a + b + c + d)
        a, b, c, d = a * scale, b * scale, c * scale, d * scale
        step *= 2
    return a / c


def local_kernel(
    dims,
    omega_ref,
    phase_ref,
    live_ref,
    u_hbm,
    source_ref,
    stencil_ref,
    coupling_ref,
    diag_ref,
    owner_ref,
    row_ref,
    work_ref,
    green_ref,
    shift_ref,
    pick_ref,
    keep_ref,
    rimw_ref,
    couple_s,
    diag_s,
    green_row,
    sum_row,
    green_col,
    sum_col,
    face_s,
    round_s,
    u_s,
    u_sems,
):
    times, cx, cz, pairs, points, count = dims
    rows = cx * cz
    span = times * pairs
    pair_now = pl.program_id(0)
    wide = couple_s.shape[1]

    trio = u_s.shape[2]

    def fetch(pair):
        lanes = pl.ds(pl.multiple_of(pair * trio, trio), trio)
        return pltpu.make_async_copy(u_hbm.at[:, lanes], u_s.at[pair], u_sems.at[pair])

    @pl.when(pair_now == 0)
    def prepare():
        for pair in range(pairs):
            fetch(pair).start()
        states = coupling_ref.shape[0]
        lane = iota((8, wide), 1)
        couple_s[...] = jnp.ones_like(couple_s)
        diag_s[...] = jnp.ones_like(diag_s)
        couple_s[0:states, 0:points] = coupling_ref[...]
        diag_s[0:states, 0:points] = diag_ref[...]
        link = couple_s[...]
        diag = diag_s[...]
        before = jnp.where(lane == 0, 0.0, pltpu.roll(link, 1, 1))
        one = jnp.ones_like(link)
        e = scan_products((diag + before, diag * before, one, before), lane, points, False)
        inside = lane < points
        matrix = (
            jnp.where(inside, diag + link, 1.0),
            jnp.where(inside, diag * link, 0.0),
            jnp.where(inside, one, 0.0),
            jnp.where(inside, link, 1.0),
        )
        f = jnp.where(inside, scan_products(matrix, lane, points, True), 1.0)
        e_before = jnp.where(lane == 0, 1.0, pltpu.roll(e, 1, 1))
        e_before = jnp.where(inside, e_before, 1.0)
        green = 1.0 / (before * e_before / (before + e_before) + f)
        decay = jnp.log(1.0 + f / jnp.where(lane == 0, 1.0, before))
        decay = jnp.where((lane == 0) | (lane >= points), 0.0, decay)
        step = 1
        while step < points:
            decay = decay + jnp.where(lane >= step, pltpu.roll(decay, step, 1), 0.0)
            step *= 2
        odd = iota((8, wide), 0) % 2 == 1
        green = jnp.where(odd, pltpu.roll(green, HALF, 1), green)
        decay = jnp.where(odd, pltpu.roll(decay, HALF, 1), decay)
        green_row[...] = green
        sum_row[...] = decay
        green_col[...] = green.T
        sum_col[...] = decay.T

        low = iota((rows, LANES), 1) < HALF
        z = iota((rows, 3 * LANES), 0) % cz
        for way in range(4):
            at = way // 2 * 3 * LANES
            t0, t1, t2 = (stencil_ref[:, at + k * LANES : at + (k + 1) * LANES] for k in range(3))
            if way % 2 == 0:
                swap = pltpu.roll(t0, HALF, 1)
                tiles = (t0, jnp.where(low, t1, swap), jnp.where(low, swap, pltpu.roll(t1, HALF, 1)))
            else:
                swap = pltpu.roll(t2, HALF, 1)
                other = pltpu.roll(t1, HALF, 1)
                tiles = (jnp.where(low, other, swap), jnp.where(low, swap, t1), t2)
            face = jnp.concatenate(tiles, 1)
            if way == 0:
                rimw_ref[0:cz, :] = face[0:cz]
            elif way == 1:
                rimw_ref[cz : 2 * cz, :] = face[rows - cz :]
            elif way == 2:
                rimw_ref[2 * cz : 2 * cz + rows, :] = jnp.where(z == 0, face, 0.0)
                face = jnp.where(z == 0, 0.0, face)
            else:
                rimw_ref[2 * cz + rows : 2 * cz + 2 * rows, :] = jnp.where(z == cz - 1, face, 0.0)
                face = jnp.where(z == cz - 1, 0.0, face)
            face_s[way * rows : (way + 1) * rows, :] = face

        slot = owner_ref[...] - lax.axis_index("stream") + (count // 2 + REACH)
        slot = jnp.where(slot < 0, slot + count, slot)
        slot = jnp.where(slot >= count, slot - count, slot)
        diagonal = iota((rows, rows), 0) == iota((rows, rows), 1)
        target = jnp.sum(jnp.where(diagonal, row_ref[...].astype(F32), 0.0), axis=1, keepdims=True)
        target = target.astype(jnp.int32)
        part = rows // GROUPS
        group = jnp.zeros_like(target)
        for k in range(1, GROUPS):
            group = group + jnp.where(target >= k * part, 1, 0)
        wanted = slot * part + target - group * part
        cell = iota((rows, OWNERS * part), 1)
        pick_ref[...] = jnp.where(cell == wanted, 1.0, 0.0).astype(BF16)
        keep_ref[...] = jnp.where(iota((rows, LANES), 1) % HALF // span == group, 1.0, 0.0)

        left = iota((LANES, LANES), 0)
        right = iota((LANES, LANES), 1)
        left_in = left % HALF
        right_in = right % HALF
        left_in_part = left_in % span
        offset = right_in // pairs - left_in_part // pairs
        angle = (2.0 * math.pi / times) * offset.astype(F32)
        total = jnp.ones((LANES, LANES), F32)
        for harmonic in range(1, (times - 1) // 2 + 1):
            total = total + 2.0 * jnp.cos(harmonic * (angle + phase_ref[0]))
        ok = (left // HALF != right // HALF) & (left_in_part % pairs == right_in % pairs)
        ok = ok & (right_in < span) & (left_in < 3 * span)
        high, low_part = split(jnp.where(ok, total / times, 0.0))
        shift_ref[0:LANES, :] = high
        shift_ref[LANES : 2 * LANES, :] = low_part

    for half in range(2):
        state = 2 * pair_now + half
        first = half * HALF
        g_row = green_row[pl.ds(state, 1), :]
        s_row = sum_row[pl.ds(state, 1), :]
        pick = iota((wide, 8), 1) == state
        g_col = jnp.sum(jnp.where(pick, green_col[...], 0.0), axis=1, keepdims=True)
        s_col = jnp.sum(jnp.where(pick, sum_col[...], 0.0), axis=1, keepdims=True)
        k = iota((wide, wide), 0)
        n = iota((wide, wide), 1)
        full = jnp.exp(-jnp.abs(s_col - s_row)) * jnp.where(k <= n, g_col, g_row)
        at_end = first + points - 1
        lane = iota((1, wide), 1)
        s_end = jnp.sum(jnp.where(lane == at_end, s_row, 0.0), axis=1, keepdims=True)
        link = couple_s[pl.ds(state, 1), :]
        c_end = jnp.sum(jnp.where(lane == points - 1, link, 0.0), axis=1, keepdims=True)
        last = c_end * jnp.exp(-jnp.abs(s_end - s_row)) * g_row
        inside_k = (k >= first) & (k < first + points)
        inside_n = (n >= first) & (n < first + points)
        inner = k % HALF
        added = (inner < span) & (inner % pairs == pair_now)
        full = jnp.where(inside_k, full, jnp.where(added, last, 0.0))
        full = jnp.where(inside_n, full, 0.0)
        high, low_part = split(full)
        green_ref[0, 2 * half] = high
        green_ref[0, 2 * half + 1] = low_part

    fetch(pair_now).wait()
    u_ref = u_s.at[pair_now]
    round_s[...] = u_ref[...].astype(BF16).astype(F32)
    omega = omega_ref[0]
    live = live_ref[0]
    z = iota((cz, 3 * LANES), 0)
    weights = []
    for n in range(1, (times - 1) // 2 + 1):
        weights.append(omega * (0.5 * (-1.0) ** n / math.sin(math.pi * n / times)))
    for x in range(cx):
        west, east, south, north = (
            face_s[way * rows + x * cz : way * rows + (x + 1) * cz, :] for way in range(4)
        )
        for t in range(times):
            at = lambda tt, xx: slice((tt % times) * rows + xx * cz, (tt % times) * rows + (xx + 1) * cz)
            here = round_s[at(t, x), :]
            value = source_ref[t, x].astype(F32)
            value += south * pltpu.roll(here, 1, 0) + north * pltpu.roll(here, cz - 1, 0)
            if x > 0:
                value += west * round_s[at(t, x - 1), :]
            if x < cx - 1:
                value += east * round_s[at(t, x + 1), :]
            for n, weight in enumerate(weights, 1):
                value -= weight * (u_ref[at(t + n, x), :] - u_ref[at(t - n, x), :])
            work_ref[at(t, x), :] = jnp.where(z + x * cz < live, value, u_ref[at(t, x), :])


def finish_kernel(
    dims,
    live_ref,
    rim_ref,
    work_ref,
    green_ref,
    shift_ref,
    pick_ref,
    keep_ref,
    rimw_ref,
    second_z_ref,
    second_x_ref,
    first_z_ref,
    first_x_ref,
    out_ref,
    rim_s,
    ghost_s,
    south_s,
    north_s,
    high_s,
    low_s,
):
    times, cx, cz, pairs, points, count = dims
    rows = cx * cz
    part = rows // GROUPS

    @pl.when(pl.program_id(0) == 0)
    def ghosts():
        ghost = jnp.zeros((rows, LANES), F32)
        for piece in range(PARTS):
            for k in range(OWNERS):
                owner = lax.rem(lax.axis_index("stream") + (count + count // 2 - REACH + k), count)
                rim_s[k * part : (k + 1) * part, :] = rim_ref[owner, piece * part : (piece + 1) * part]
            picked = jnp.dot(pick_ref[...], rim_s[...], preferred_element_type=F32)
            picked = (picked * keep_ref[...]).astype(BF16)
            ghost += jnp.dot(picked, shift_ref[0:LANES, :], preferred_element_type=F32)
            ghost += jnp.dot(picked, shift_ref[LANES : 2 * LANES, :], preferred_element_type=F32)
        ghost_s[...] = ghost

    first = first_x_ref[...].astype(F32)
    second = second_x_ref[...].astype(F32)
    even_x = lax.axis_index("stream") % 2 == 0
    west = jnp.where(even_x, second, first)
    east = jnp.where(even_x, first, second)
    first = first_z_ref[...].astype(F32)
    second = second_z_ref[...].astype(F32)
    even_z = lax.axis_index("span") % 2 == 0
    south_s[...] = jnp.where(even_z, second, first)
    north_s[...] = jnp.where(even_z, first, second)
    lane = iota((cz, LANES), 1)
    inner = lane % HALF
    low_half = lane < HALF
    for t in range(times):
        mine = (inner >= t * pairs) & (inner < (t + 1) * pairs)
        even, odd = [], []
        for x in range(cx):
            at = t * rows + x * cz
            value = work_ref[at : at + cz, :]
            if x == 0:
                value += rimw_ref[0:cz, :] * west[t * cz : (t + 1) * cz]
            if x == cx - 1:
                value += rimw_ref[cz : 2 * cz, :] * east[t * cz : (t + 1) * cz]
            south = rimw_ref[2 * cz + x * cz : 2 * cz + (x + 1) * cz, :]
            north = rimw_ref[2 * cz + rows + x * cz : 2 * cz + rows + (x + 1) * cz, :]
            value += south * south_s[x * 8 + t : x * 8 + t + 1, :]
            value += north * north_s[x * 8 + t : x * 8 + t + 1, :]
            ghost = jnp.where(mine, ghost_s[x * cz : (x + 1) * cz, :], 0.0)
            mid = value[:, LANES : 2 * LANES]
            even.append(jnp.concatenate([value[:, :LANES], jnp.where(low_half, mid, ghost)], 1))
            odd.append(jnp.concatenate([jnp.where(low_half, ghost, mid), value[:, 2 * LANES :]], 1))
        for half, pieces in ((0, even), (1, odd)):
            high, low = split(jnp.concatenate(pieces, 0))
            high_s[half, t * rows : (t + 1) * rows, :] = high
            low_s[half, t * rows : (t + 1) * rows, :] = low
    products = []
    for half in range(2):
        high = high_s[half]
        g_high = green_ref[0, 2 * half]
        total = jnp.dot(high, g_high, preferred_element_type=F32)
        total += jnp.dot(high, green_ref[0, 2 * half + 1], preferred_element_type=F32)
        total += jnp.dot(low_s[half], g_high, preferred_element_type=F32)
        products.append(total)
    even, odd = products
    tiles = (even[:, :LANES], even[:, LANES:] + odd[:, :LANES], odd[:, LANES:])
    live = live_ref[0]
    shape = out_ref.shape[:1] + (LANES,)
    alive = iota(shape, 0) % rows < live
    for k, tile in enumerate(tiles):
        lanes = slice(k * LANES, (k + 1) * LANES)
        out_ref[:, lanes] = jnp.where(alive, tile, work_ref[:, lanes])


def pairing(count, first):
    up = [(i, i + 1) for i in range(first, count - 1, 2)]
    return up + [(b, a) for a, b in up]


def body(
    adjoint,
    source,
    stencil,
    line_coupling,
    line_diag,
    omega,
    phase,
    match_owner,
    match_row,
    tile_live,
):
    times, cx, cz, width = adjoint.shape
    states, points = line_coupling.shape
    pairs = states // 2
    rows = cx * cz
    lines = times * rows
    count = lax.axis_size("stream")
    spans = lax.axis_size("span")
    wide = 2 * LANES
    u = adjoint.reshape(lines, width)
    vmem = pl.BlockSpec(memory_space=pltpu.VMEM)
    smem = pl.BlockSpec(memory_space=pltpu.SMEM)
    part = rows // GROUPS
    rim, second_z, second_x, first_z, first_x = pl.pallas_call(
        functools.partial(edge_kernel, (times, cx, cz, pairs)),
        out_shape=(
            jax.ShapeDtypeStruct((count, PARTS * part, LANES), BF16),
            jax.ShapeDtypeStruct((cx * 8, width), BF16),
            jax.ShapeDtypeStruct((times * cz, width), BF16),
            jax.ShapeDtypeStruct((cx * 8, width), BF16),
            jax.ShapeDtypeStruct((times * cz, width), BF16),
        ),
        in_specs=[vmem],
        out_specs=(vmem,) * 5,
        compiler_params=pltpu.CompilerParams(vmem_limit_bytes=VMEM_GRANT),
        name="edges",
    )(u)

    rims = lax.all_to_all(rim, "stream", 0, 0)
    second_z = lax.ppermute(second_z, "span", pairing(spans, 1))
    second_x = lax.ppermute(second_x, "stream", pairing(count, 1))
    first_x = lax.ppermute(first_x, "stream", pairing(count, 0))
    first_z = lax.ppermute(first_z, "span", pairing(spans, 0))

    live = tile_live.reshape(1)
    trio = 3 * LANES
    rim_rows = 2 * cz + 2 * rows
    work, green, shift, pick, keep, rim_weights = pl.pallas_call(
        functools.partial(local_kernel, (times, cx, cz, pairs, points, count)),
        out_shape=(
            pltpu.HBM((lines, width), F32),
            pltpu.HBM((pairs, 4, wide, wide), BF16),
            pltpu.HBM((2 * LANES, LANES), BF16),
            pltpu.HBM((rows, OWNERS * part), BF16),
            pltpu.HBM((rows, LANES), F32),
            pltpu.HBM((rim_rows, trio), F32),
        ),
        grid=(pairs,),
        in_specs=[
            smem,
            smem,
            smem,
            pl.BlockSpec(memory_space=pltpu.HBM),
            pl.BlockSpec((times, cx, cz, trio), lambda p: (0, 0, 0, p)),
            pl.BlockSpec((rows, 4 * points), lambda p: (0, 0)),
            pl.BlockSpec((states, points), lambda p: (0, 0)),
            pl.BlockSpec((states, points), lambda p: (0, 0)),
            pl.BlockSpec((rows, 1), lambda p: (0, 0)),
            pl.BlockSpec((1, rows), lambda p: (0, 0)),
        ],
        out_specs=(
            pl.BlockSpec((lines, trio), lambda p: (0, p)),
            pl.BlockSpec((1, 4, wide, wide), lambda p: (p, 0, 0, 0)),
            pl.BlockSpec((2 * LANES, LANES), lambda p: (0, 0)),
            pl.BlockSpec((rows, OWNERS * part), lambda p: (0, 0)),
            pl.BlockSpec((rows, LANES), lambda p: (0, 0)),
            pl.BlockSpec((rim_rows, trio), lambda p: (0, 0)),
        ),
        scratch_shapes=[
            pltpu.VMEM((8, wide), F32),
            pltpu.VMEM((8, wide), F32),
            pltpu.VMEM((8, wide), F32),
            pltpu.VMEM((8, wide), F32),
            pltpu.VMEM((wide, 8), F32),
            pltpu.VMEM((wide, 8), F32),
            pltpu.VMEM((4 * rows, trio), F32),
            pltpu.VMEM((lines, trio), F32),
            pltpu.VMEM((pairs, lines, trio), F32),
            pltpu.SemaphoreType.DMA((pairs,)),
        ],
        compiler_params=pltpu.CompilerParams(vmem_limit_bytes=52 * 2**20),
        cost_estimate=pl.CostEstimate(flops=20_000_000, bytes_accessed=6_000_000, transcendentals=400_000),
        name="local",
    )(
        omega,
        phase,
        live,
        u,
        source,
        stencil.reshape(rows, 4 * points),
        line_coupling,
        line_diag,
        match_owner.reshape(rows, 1),
        match_row.reshape(1, rows),
    )

    whole = lambda array: pl.BlockSpec(array.shape, lambda p: (0, 0))
    edge = lambda array: pl.BlockSpec((array.shape[0], trio), lambda p: (0, p))
    updated = pl.pallas_call(
        functools.partial(finish_kernel, (times, cx, cz, pairs, points, count)),
        out_shape=jax.ShapeDtypeStruct((lines, width), F32),
        grid=(pairs,),
        in_specs=[
            smem,
            pl.BlockSpec(rims.shape, lambda p: (0, 0, 0)),
            edge(work),
            pl.BlockSpec((1, 4, wide, wide), lambda p: (p, 0, 0, 0)),
            whole(shift),
            whole(pick),
            whole(keep),
            whole(rim_weights),
            edge(second_z),
            edge(second_x),
            edge(first_z),
            edge(first_x),
        ],
        out_specs=edge(work),
        scratch_shapes=[
            pltpu.VMEM((OWNERS * part, LANES), BF16),
            pltpu.VMEM((rows, LANES), F32),
            pltpu.VMEM((cx * 8, trio), F32),
            pltpu.VMEM((cx * 8, trio), F32),
            pltpu.VMEM((2, lines, wide), BF16),
            pltpu.VMEM((2, lines, wide), BF16),
        ],
        compiler_params=pltpu.CompilerParams(vmem_limit_bytes=65400 * 2**10),
        cost_estimate=pl.CostEstimate(flops=800_000_000, bytes_accessed=5_000_000, transcendentals=0),
        name="finish",
    )(
        live,
        rims,
        work,
        green,
        shift,
        pick,
        keep,
        rim_weights,
        second_z,
        second_x,
        first_z,
        first_x,
    )
    return updated.reshape(times, cx, cz, width)


def solution(mesh):
    in_specs = (
        P(None, "stream", "span", None),
        P(None, "stream", "span", None),
        P("stream", "span", None),
        P(),
        P(),
        P(),
        P(),
        P("stream", "span", None, None),
        P("stream", "span", None),
        P("stream", "span"),
    )
    out_specs = P(None, "stream", "span", None)
    return jax.shard_map(body, mesh=mesh, in_specs=in_specs, out_specs=out_specs, check_vma=False)
```

```python
import functools
import math

import jax
import jax.numpy as jnp
from jax import lax
from jax.experimental import pallas as pl
from jax.experimental.pallas import tpu as pltpu
from jax.sharding import PartitionSpec as P

F32 = jnp.float32
BF16 = jnp.bfloat16
LANES = 128
HALF = 64
REACH = 3
OWNERS = 8
VMEM_GRANT = 60 * 2**20
GROUPS = 3
PARTS = 1


def iota(shape, dim):
    return lax.broadcasted_iota(jnp.int32, shape, dim)


def split(value):
    high = value.astype(BF16)
    return high, (value - high.astype(F32)).astype(BF16)


def edge_kernel(
    dims, u_hbm, rim_ref, second_z_ref, second_x_ref, first_z_ref, first_x_ref, u_ref, u_sems
):
    times, cx, cz, pairs = dims
    rows = cx * cz
    trio = u_ref.shape[1] // pairs
    spans = [slice(pair * trio, (pair + 1) * trio) for pair in range(pairs)]
    fetches = [
        pltpu.make_async_copy(u_hbm.at[:, lanes], u_ref.at[:, lanes], u_sems.at[pair])
        for pair, lanes in enumerate(spans)
    ]
    for fetch in fetches:
        fetch.start()
    even_x = lax.axis_index("stream") % 2 == 0
    even_z = lax.axis_index("span") % 2 == 0
    top = cz - 1
    sub = iota((8, trio), 0)
    lane = iota((rows, LANES), 1)
    inner = lane % HALF
    span = times * pairs
    found = jnp.zeros((rows, LANES), F32)
    for pair, lanes in enumerate(spans):
        fetches[pair].wait()
        base = pair * trio
        for t in range(times):
            block = slice(t * rows, (t + 1) * rows)
            first = u_ref[block, base + LANES : base + 2 * LANES]
            second = u_ref[block, base + 2 * LANES : base + 3 * LANES]
            both = jnp.where(lane < HALF, first, second)
            spot = t * pairs + pair
            both = pltpu.roll(both, (spot - (HALF - 1)) % LANES, 1)
            found = jnp.where(inner == spot, both, found)
        take = lambda t, x: u_ref[t * rows + x * cz : t * rows + x * cz + cz, lanes]
        west = jnp.concatenate([take(t, 0) for t in range(times)], 0)
        east = jnp.concatenate([take(t, cx - 1) for t in range(times)], 0)
        first_x_ref[:, lanes] = jnp.where(even_x, east, west).astype(BF16)
        second_x_ref[:, lanes] = jnp.where(even_x, west, east).astype(BF16)
        for ref, z in (
            (first_z_ref, jnp.where(even_z, top, 0)),
            (second_z_ref, jnp.where(even_z, 0, top)),
        ):
            tiles = []
            for x in range(cx):
                tile = jnp.zeros((8, trio), F32)
                for t in range(times):
                    tile = jnp.where(sub == t, u_ref[pl.ds(t * rows + x * cz + z, 1), lanes], tile)
                tiles.append(tile)
            ref[:, lanes] = jnp.concatenate(tiles, 0).astype(BF16)
    part = rows // GROUPS
    parts = []
    for _ in range(PARTS):
        rounded = found.astype(BF16).astype(F32)
        found = found - rounded
        packed = rounded[:part]
        for group in range(1, GROUPS):
            packed = packed + pltpu.roll(rounded[group * part : (group + 1) * part], group * span, 1)
        parts.append(packed)
    packed = jnp.concatenate(parts, 0).astype(BF16)
    for other in range(rim_ref.shape[0]):
        rim_ref[other] = packed


def scan_products(matrix, lane, points, backward):
    a, b, c, d = matrix
    step = 1
    while step < points:
        shift = (lane.shape[1] - step) if backward else step
        inside = (lane < points - step) if backward else (lane >= step)
        e = jnp.where(inside, pltpu.roll(a, shift, 1), 1.0)
        f = jnp.where(inside, pltpu.roll(b, shift, 1), 0.0)
        g = jnp.where(inside, pltpu.roll(c, shift, 1), 0.0)
        h = jnp.where(inside, pltpu.roll(d, shift, 1), 1.0)
        a, b, c, d = a * e + b * g, a * f + b * h, c * e + d * g, c * f + d * h
        scale = 1.0 / (a + b + c + d)
        a, b, c, d = a * scale, b * scale, c * scale, d * scale
        step *= 2
    return a / c


def local_kernel(
    dims,
    omega_ref,
    phase_ref,
    live_ref,
    u_hbm,
    source_ref,
    stencil_ref,
    coupling_ref,
    diag_ref,
    owner_ref,
    row_ref,
    work_ref,
    couple_s,
    green_row,
    sum_row,
    green_col,
    sum_col,
    shift_ref,
    pick_ref,
    keep_ref,
    rimw_ref,
    diag_s,
    face_s,
    round_s,
    u_s,
    u_sems,
):
    times, cx, cz, pairs, points, count = dims
    rows = cx * cz
    span = times * pairs
    pair_now = pl.program_id(0)
    wide = couple_s.shape[1]

    trio = u_s.shape[2]

    def fetch(pair):
        lanes = pl.ds(pl.multiple_of(pair * trio, trio), trio)
        return pltpu.make_async_copy(u_hbm.at[:, lanes], u_s.at[pair], u_sems.at[pair])

    @pl.when(pair_now == 0)
    def prepare():
        for pair in range(pairs):
            fetch(pair).start()
        states = coupling_ref.shape[0]
        lane = iota((8, wide), 1)
        couple_s[...] = jnp.ones_like(couple_s)
        diag_s[...] = jnp.ones_like(diag_s)
        couple_s[0:states, 0:points] = coupling_ref[...]
        diag_s[0:states, 0:points] = diag_ref[...]
        link = couple_s[...]
        diag = diag_s[...]
        before = jnp.where(lane == 0, 0.0, pltpu.roll(link, 1, 1))
        one = jnp.ones_like(link)
        e = scan_products((diag + before, diag * before, one, before), lane, points, False)
        inside = lane < points
        matrix = (
            jnp.where(inside, diag + link, 1.0),
            jnp.where(inside, diag * link, 0.0),
            jnp.where(inside, one, 0.0),
            jnp.where(inside, link, 1.0),
        )
        f = jnp.where(inside, scan_products(matrix, lane, points, True), 1.0)
        e_before = jnp.where(lane == 0, 1.0, pltpu.roll(e, 1, 1))
        e_before = jnp.where(inside, e_before, 1.0)
        green = 1.0 / (before * e_before / (before + e_before) + f)
        decay = jnp.log(1.0 + f / jnp.where(lane == 0, 1.0, before))
        decay = jnp.where((lane == 0) | (lane >= points), 0.0, decay)
        step = 1
        while step < points:
            decay = decay + jnp.where(lane >= step, pltpu.roll(decay, step, 1), 0.0)
            step *= 2
        odd = iota((8, wide), 0) % 2 == 1
        green = jnp.where(odd, pltpu.roll(green, HALF, 1), green)
        decay = jnp.where(odd, pltpu.roll(decay, HALF, 1), decay)
        green_row[...] = green
        sum_row[...] = decay
        green_col[...] = green.T
        sum_col[...] = decay.T

        low = iota((rows, LANES), 1) < HALF
        z = iota((rows, 3 * LANES), 0) % cz
        for way in range(4):
            at = way // 2 * 3 * LANES
            t0, t1, t2 = (stencil_ref[:, at + k * LANES : at + (k + 1) * LANES] for k in range(3))
            if way % 2 == 0:
                swap = pltpu.roll(t0, HALF, 1)
                tiles = (t0, jnp.where(low, t1, swap), jnp.where(low, swap, pltpu.roll(t1, HALF, 1)))
            else:
                swap = pltpu.roll(t2, HALF, 1)
                other = pltpu.roll(t1, HALF, 1)
                tiles = (jnp.where(low, other, swap), jnp.where(low, swap, t1), t2)
            face = jnp.concatenate(tiles, 1)
            if way == 0:
                rimw_ref[0:cz, :] = face[0:cz]
            elif way == 1:
                rimw_ref[cz : 2 * cz, :] = face[rows - cz :]
            elif way == 2:
                rimw_ref[2 * cz : 2 * cz + rows, :] = jnp.where(z == 0, face, 0.0)
                face = jnp.where(z == 0, 0.0, face)
            else:
                rimw_ref[2 * cz + rows : 2 * cz + 2 * rows, :] = jnp.where(z == cz - 1, face, 0.0)
                face = jnp.where(z == cz - 1, 0.0, face)
            face_s[way * rows : (way + 1) * rows, :] = face

        slot = owner_ref[...] - lax.axis_index("stream") + (count // 2 + REACH)
        slot = jnp.where(slot < 0, slot + count, slot)
        slot = jnp.where(slot >= count, slot - count, slot)
        diagonal = iota((rows, rows), 0) == iota((rows, rows), 1)
        target = jnp.sum(jnp.where(diagonal, row_ref[...].astype(F32), 0.0), axis=1, keepdims=True)
        target = target.astype(jnp.int32)
        part = rows // GROUPS
        group = jnp.zeros_like(target)
        for k in range(1, GROUPS):
            group = group + jnp.where(target >= k * part, 1, 0)
        wanted = slot * part + target - group * part
        cell = iota((rows, OWNERS * part), 1)
        pick_ref[...] = jnp.where(cell == wanted, 1.0, 0.0).astype(BF16)
        keep_ref[...] = jnp.where(iota((rows, LANES), 1) % HALF // span == group, 1.0, 0.0)

        left = iota((LANES, LANES), 0)
        right = iota((LANES, LANES), 1)
        left_in = left % HALF
        right_in = right % HALF
        left_in_part = left_in % span
        offset = right_in // pairs - left_in_part // pairs
        angle = (2.0 * math.pi / times) * offset.astype(F32)
        total = jnp.ones((LANES, LANES), F32)
        for harmonic in range(1, (times - 1) // 2 + 1):
            total = total + 2.0 * jnp.cos(harmonic * (angle + phase_ref[0]))
        ok = (left // HALF != right // HALF) & (left_in_part % pairs == right_in % pairs)
        ok = ok & (right_in < span) & (left_in < 3 * span)
        high, low_part = split(jnp.where(ok, total / times, 0.0))
        shift_ref[0:LANES, :] = high
        shift_ref[LANES : 2 * LANES, :] = low_part

    fetch(pair_now).wait()
    u_ref = u_s.at[pair_now]
    round_s[...] = u_ref[...].astype(BF16).astype(F32)
    omega = omega_ref[0]
    live = live_ref[0]
    z = iota((cz, 3 * LANES), 0)
    weights = []
    for n in range(1, (times - 1) // 2 + 1):
        weights.append(omega * (0.5 * (-1.0) ** n / math.sin(math.pi * n / times)))
    for x in range(cx):
        west, east, south, north = (
            face_s[way * rows + x * cz : way * rows + (x + 1) * cz, :] for way in range(4)
        )
        for t in range(times):
            at = lambda tt, xx: slice((tt % times) * rows + xx * cz, (tt % times) * rows + (xx + 1) * cz)
            here = round_s[at(t, x), :]
            value = source_ref[t, x].astype(F32)
            value += south * pltpu.roll(here, 1, 0) + north * pltpu.roll(here, cz - 1, 0)
            if x > 0:
                value += west * round_s[at(t, x - 1), :]
            if x < cx - 1:
                value += east * round_s[at(t, x + 1), :]
            for n, weight in enumerate(weights, 1):
                value -= weight * (u_ref[at(t + n, x), :] - u_ref[at(t - n, x), :])
            work_ref[at(t, x), :] = jnp.where(z + x * cz < live, value, u_ref[at(t, x), :])


def finish_kernel(
    dims,
    live_ref,
    rim_ref,
    work_ref,
    couple_s,
    green_row,
    sum_row,
    green_col,
    sum_col,
    shift_ref,
    pick_ref,
    keep_ref,
    rimw_ref,
    second_z_ref,
    second_x_ref,
    first_z_ref,
    first_x_ref,
    out_ref,
    rim_s,
    ghost_s,
    south_s,
    north_s,
    high_s,
    low_s,
):
    times, cx, cz, pairs, points, count = dims
    rows = cx * cz
    part = rows // GROUPS

    @pl.when(pl.program_id(0) == 0)
    def ghosts():
        ghost = jnp.zeros((rows, LANES), F32)
        for piece in range(PARTS):
            for k in range(OWNERS):
                owner = lax.rem(lax.axis_index("stream") + (count + count // 2 - REACH + k), count)
                rim_s[k * part : (k + 1) * part, :] = rim_ref[owner, piece * part : (piece + 1) * part]
            picked = jnp.dot(pick_ref[...], rim_s[...], preferred_element_type=F32)
            picked = (picked * keep_ref[...]).astype(BF16)
            ghost += jnp.dot(picked, shift_ref[0:LANES, :], preferred_element_type=F32)
            ghost += jnp.dot(picked, shift_ref[LANES : 2 * LANES, :], preferred_element_type=F32)
        ghost_s[...] = ghost

    first = first_x_ref[...].astype(F32)
    second = second_x_ref[...].astype(F32)
    even_x = lax.axis_index("stream") % 2 == 0
    west = jnp.where(even_x, second, first)
    east = jnp.where(even_x, first, second)
    first = first_z_ref[...].astype(F32)
    second = second_z_ref[...].astype(F32)
    even_z = lax.axis_index("span") % 2 == 0
    south_s[...] = jnp.where(even_z, second, first)
    north_s[...] = jnp.where(even_z, first, second)
    lane = iota((cz, LANES), 1)
    inner = lane % HALF
    low_half = lane < HALF
    for t in range(times):
        mine = (inner >= t * pairs) & (inner < (t + 1) * pairs)
        even, odd = [], []
        for x in range(cx):
            at = t * rows + x * cz
            value = work_ref[at : at + cz, :]
            if x == 0:
                value += rimw_ref[0:cz, :] * west[t * cz : (t + 1) * cz]
            if x == cx - 1:
                value += rimw_ref[cz : 2 * cz, :] * east[t * cz : (t + 1) * cz]
            south = rimw_ref[2 * cz + x * cz : 2 * cz + (x + 1) * cz, :]
            north = rimw_ref[2 * cz + rows + x * cz : 2 * cz + rows + (x + 1) * cz, :]
            value += south * south_s[x * 8 + t : x * 8 + t + 1, :]
            value += north * north_s[x * 8 + t : x * 8 + t + 1, :]
            ghost = jnp.where(mine, ghost_s[x * cz : (x + 1) * cz, :], 0.0)
            mid = value[:, LANES : 2 * LANES]
            even.append(jnp.concatenate([value[:, :LANES], jnp.where(low_half, mid, ghost)], 1))
            odd.append(jnp.concatenate([jnp.where(low_half, ghost, mid), value[:, 2 * LANES :]], 1))
        for half, pieces in ((0, even), (1, odd)):
            high, low = split(jnp.concatenate(pieces, 0))
            high_s[half, t * rows : (t + 1) * rows, :] = high
            low_s[half, t * rows : (t + 1) * rows, :] = low
    pair_now = pl.program_id(0)
    span = times * pairs
    wide = couple_s.shape[1]
    inverses = []
    for half in range(2):
        state = 2 * pair_now + half
        first = half * HALF
        g_row = green_row[pl.ds(state, 1), :]
        s_row = sum_row[pl.ds(state, 1), :]
        pick = iota((wide, 8), 1) == state
        g_col = jnp.sum(jnp.where(pick, green_col[...], 0.0), axis=1, keepdims=True)
        s_col = jnp.sum(jnp.where(pick, sum_col[...], 0.0), axis=1, keepdims=True)
        k = iota((wide, wide), 0)
        n = iota((wide, wide), 1)
        full = jnp.exp(-jnp.abs(s_col - s_row)) * jnp.where(k <= n, g_col, g_row)
        at_end = first + points - 1
        lane = iota((1, wide), 1)
        s_end = jnp.sum(jnp.where(lane == at_end, s_row, 0.0), axis=1, keepdims=True)
        link = couple_s[pl.ds(state, 1), :]
        c_end = jnp.sum(jnp.where(lane == points - 1, link, 0.0), axis=1, keepdims=True)
        last = c_end * jnp.exp(-jnp.abs(s_end - s_row)) * g_row
        inside_k = (k >= first) & (k < first + points)
        inside_n = (n >= first) & (n < first + points)
        spot = k % HALF
        added = (spot < span) & (spot % pairs == pair_now)
        full = jnp.where(inside_k, full, jnp.where(added, last, 0.0))
        full = jnp.where(inside_n, full, 0.0)
        high, low_part = split(full)
        inverses.append((high, low_part))
    products = []
    for half in range(2):
        high = high_s[half]
        g_high, g_low = inverses[half]
        total = jnp.dot(high, g_high, preferred_element_type=F32)
        total += jnp.dot(high, g_low, preferred_element_type=F32)
        total += jnp.dot(low_s[half], g_high, preferred_element_type=F32)
        products.append(total)
    even, odd = products
    tiles = (even[:, :LANES], even[:, LANES:] + odd[:, :LANES], odd[:, LANES:])
    live = live_ref[0]
    shape = out_ref.shape[:1] + (LANES,)
    alive = iota(shape, 0) % rows < live
    for k, tile in enumerate(tiles):
        lanes = slice(k * LANES, (k + 1) * LANES)
        out_ref[:, lanes] = jnp.where(alive, tile, work_ref[:, lanes])


def pairing(count, first):
    up = [(i, i + 1) for i in range(first, count - 1, 2)]
    return up + [(b, a) for a, b in up]


def body(
    adjoint,
    source,
    stencil,
    line_coupling,
    line_diag,
    omega,
    phase,
    match_owner,
    match_row,
    tile_live,
):
    times, cx, cz, width = adjoint.shape
    states, points = line_coupling.shape
    pairs = states // 2
    rows = cx * cz
    lines = times * rows
    count = lax.axis_size("stream")
    spans = lax.axis_size("span")
    wide = 2 * LANES
    u = adjoint.reshape(lines, width)
    vmem = pl.BlockSpec(memory_space=pltpu.VMEM)
    smem = pl.BlockSpec(memory_space=pltpu.SMEM)
    part = rows // GROUPS
    rim, second_z, second_x, first_z, first_x = pl.pallas_call(
        functools.partial(edge_kernel, (times, cx, cz, pairs)),
        out_shape=(
            jax.ShapeDtypeStruct((count, PARTS * part, LANES), BF16),
            jax.ShapeDtypeStruct((cx * 8, width), BF16),
            jax.ShapeDtypeStruct((times * cz, width), BF16),
            jax.ShapeDtypeStruct((cx * 8, width), BF16),
            jax.ShapeDtypeStruct((times * cz, width), BF16),
        ),
        in_specs=[pl.BlockSpec(memory_space=pltpu.HBM)],
        out_specs=(vmem,) * 5,
        scratch_shapes=[pltpu.VMEM((lines, width), F32), pltpu.SemaphoreType.DMA((pairs,))],
        compiler_params=pltpu.CompilerParams(vmem_limit_bytes=VMEM_GRANT),
        name="edges",
    )(u)

    rims = lax.all_to_all(rim, "stream", 0, 0)
    second_z = lax.ppermute(second_z, "span", pairing(spans, 1))
    second_x = lax.ppermute(second_x, "stream", pairing(count, 1))
    first_x = lax.ppermute(first_x, "stream", pairing(count, 0))
    first_z = lax.ppermute(first_z, "span", pairing(spans, 0))

    live = tile_live.reshape(1)
    trio = 3 * LANES
    rim_rows = 2 * cz + 2 * rows
    work, couple, green_row, sum_row, green_col, sum_col, shift, pick, keep, rim_weights = pl.pallas_call(
        functools.partial(local_kernel, (times, cx, cz, pairs, points, count)),
        out_shape=(
            pltpu.HBM((lines, width), F32),
            pltpu.HBM((8, wide), F32),
            pltpu.HBM((8, wide), F32),
            pltpu.HBM((8, wide), F32),
            pltpu.HBM((wide, 8), F32),
            pltpu.HBM((wide, 8), F32),
            pltpu.HBM((2 * LANES, LANES), BF16),
            pltpu.HBM((rows, OWNERS * part), BF16),
            pltpu.HBM((rows, LANES), F32),
            pltpu.HBM((rim_rows, trio), F32),
        ),
        grid=(pairs,),
        in_specs=[
            smem,
            smem,
            smem,
            pl.BlockSpec(memory_space=pltpu.HBM),
            pl.BlockSpec((times, cx, cz, trio), lambda p: (0, 0, 0, p)),
            pl.BlockSpec((rows, 4 * points), lambda p: (0, 0)),
            pl.BlockSpec((states, points), lambda p: (0, 0)),
            pl.BlockSpec((states, points), lambda p: (0, 0)),
            pl.BlockSpec((rows, 1), lambda p: (0, 0)),
            pl.BlockSpec((1, rows), lambda p: (0, 0)),
        ],
        out_specs=(
            pl.BlockSpec((lines, trio), lambda p: (0, p)),
            pl.BlockSpec((8, wide), lambda p: (0, 0)),
            pl.BlockSpec((8, wide), lambda p: (0, 0)),
            pl.BlockSpec((8, wide), lambda p: (0, 0)),
            pl.BlockSpec((wide, 8), lambda p: (0, 0)),
            pl.BlockSpec((wide, 8), lambda p: (0, 0)),
            pl.BlockSpec((2 * LANES, LANES), lambda p: (0, 0)),
            pl.BlockSpec((rows, OWNERS * part), lambda p: (0, 0)),
            pl.BlockSpec((rows, LANES), lambda p: (0, 0)),
            pl.BlockSpec((rim_rows, trio), lambda p: (0, 0)),
        ),
        scratch_shapes=[
            pltpu.VMEM((8, wide), F32),
            pltpu.VMEM((4 * rows, trio), F32),
            pltpu.VMEM((lines, trio), F32),
            pltpu.VMEM((pairs, lines, trio), F32),
            pltpu.SemaphoreType.DMA((pairs,)),
        ],
        compiler_params=pltpu.CompilerParams(vmem_limit_bytes=52 * 2**20),
        cost_estimate=pl.CostEstimate(flops=20_000_000, bytes_accessed=6_000_000, transcendentals=400_000),
        name="local",
    )(
        omega,
        phase,
        live,
        u,
        source,
        stencil.reshape(rows, 4 * points),
        line_coupling,
        line_diag,
        match_owner.reshape(rows, 1),
        match_row.reshape(1, rows),
    )

    whole = lambda array: pl.BlockSpec(array.shape, lambda p: (0, 0))
    edge = lambda array: pl.BlockSpec((array.shape[0], trio), lambda p: (0, p))
    updated = pl.pallas_call(
        functools.partial(finish_kernel, (times, cx, cz, pairs, points, count)),
        out_shape=jax.ShapeDtypeStruct((lines, width), F32),
        grid=(pairs,),
        in_specs=[
            smem,
            pl.BlockSpec(rims.shape, lambda p: (0, 0, 0)),
            edge(work),
            pl.BlockSpec((8, wide), lambda p: (0, 0)),
            pl.BlockSpec((8, wide), lambda p: (0, 0)),
            pl.BlockSpec((8, wide), lambda p: (0, 0)),
            pl.BlockSpec((wide, 8), lambda p: (0, 0)),
            pl.BlockSpec((wide, 8), lambda p: (0, 0)),
            whole(shift),
            whole(pick),
            whole(keep),
            whole(rim_weights),
            edge(second_z),
            edge(second_x),
            edge(first_z),
            edge(first_x),
        ],
        out_specs=edge(work),
        scratch_shapes=[
            pltpu.VMEM((OWNERS * part, LANES), BF16),
            pltpu.VMEM((rows, LANES), F32),
            pltpu.VMEM((cx * 8, trio), F32),
            pltpu.VMEM((cx * 8, trio), F32),
            pltpu.VMEM((2, lines, wide), BF16),
            pltpu.VMEM((2, lines, wide), BF16),
        ],
        compiler_params=pltpu.CompilerParams(vmem_limit_bytes=65400 * 2**10),
        cost_estimate=pl.CostEstimate(flops=800_000_000, bytes_accessed=5_000_000, transcendentals=0),
        name="finish",
    )(
        live,
        rims,
        work,
        couple,
        green_row,
        sum_row,
        green_col,
        sum_col,
        shift,
        pick,
        keep,
        rim_weights,
        second_z,
        second_x,
        first_z,
        first_x,
    )
    return updated.reshape(times, cx, cz, width)


def solution(mesh):
    in_specs = (
        P(None, "stream", "span", None),
        P(None, "stream", "span", None),
        P("stream", "span", None),
        P(),
        P(),
        P(),
        P(),
        P("stream", "span", None, None),
        P("stream", "span", None),
        P("stream", "span"),
    )
    out_specs = P(None, "stream", "span", None)
    return jax.shard_map(body, mesh=mesh, in_specs=in_specs, out_specs=out_specs, check_vma=False)
```
